512 devices in a mesh: row: 64 (over x, z, core), col: 8 (over y).
Axes of the slice: x: 4, y: 8, z: 8, core: 2. Of those that a mesh axis runs over, the one named last changes fastest.
Arguments:
- eig_slab: float32 [32768, 4096], P('row', 'col'), may hold values from -6 to 6
- reflectors: float32 [16, 32768], P('col', 'row'), may hold values from -6 to 6
- row_offsets: int32 [16], replicated, may hold values from 1 to 24, as said below
Outputs:
- rotated: float32 [32768, 4096], P('row', 'col')
The draws below stay inside these ranges and needn't reach their ends.
Inputs may be any that keep to these rules, and one draw needn't show every extreme that they name: row_offsets[0] is 1; each next one is 1 or 2 larger than the one before, and exactly 8 of these steps are 2.
All inputs are finite; a program needn't handle non-finite values.
Results may differ from the reference program's by a relative error of at most 0.00027.
Values sent between devices are 32-bit elements; how exact they have to be, the bound alone decides.
A program may use at most 64 MiB of HBM per device.

```python
import math
import jax
import jax.numpy as jnp
from jax import lax

NCOLS = 4096
WIDTH = 64
SWEEPS = 16
NROWS = 32768


def shared_offsets(key):
    order_key = jax.random.fold_in(key, 7)
    order = jax.random.permutation(order_key, SWEEPS - 1)
    steps_up = 1 + (order < SWEEPS // 2).astype(jnp.int32)
    later = 1 + jnp.cumsum(steps_up).astype(jnp.int32)
    return jnp.concatenate([jnp.ones((1,), jnp.int32), later]).astype(jnp.int32)


def draw_row_offsets(key, part):
    return shared_offsets(key)


def draw_reflectors(key, part):
    offsets = shared_offsets(key)
    key = jax.random.fold_in(key, 11)
    values = jnp.clip(jax.random.normal(key, (SWEEPS, NROWS), jnp.float32), -6.0, 6.0)
    rows_all = jnp.arange(NROWS, dtype=jnp.int32)
    phase = jnp.mod(rows_all[None, :] - offsets[:, None], WIDTH)
    heavy = (phase <= 1) | (phase >= WIDTH - 2)
    weights = jnp.where(heavy, jnp.float32(1.0), jnp.float32(0.02))
    return (values * weights).astype(jnp.float32)


def block_levels(rng, shape, split, smallest, high):
    factor_of = 1.0
    for position, blocks in split:
        heights = jax.random.uniform(jax.random.fold_in(jax.random.fold_in(rng, 6), position), (blocks,), jnp.float32, smallest / len(split), high / len(split))
        factor_of = factor_of * jnp.repeat(jnp.exp(heights), shape[position] // blocks).reshape((-1,) + (1,) * (len(shape) - 1 - position))
    return factor_of


def scatter_about(own_key, extent, deviation, most, pieces=(), kind=jnp.bfloat16):
    gain = block_levels(own_key, extent, pieces, -0.22, 0.18) if pieces else 1.0
    values = jax.random.normal(own_key, extent, jnp.float32) * deviation * gain
    return jnp.minimum(jnp.maximum(values, -most), most).astype(kind)


def setup_inputs(seed: int = 0) -> dict:
    key_list = jax.random.split(jax.random.key(seed), 4)
    eig_slab = scatter_about(key_list[0], (NROWS, NCOLS), 1.0, 6.0, ((0, 64), (1, 8)), jnp.float32)
    reflectors = draw_reflectors(jax.random.fold_in(key_list[3], 71), 0)
    row_offsets = draw_row_offsets(jax.random.fold_in(key_list[3], 71), 0)
    return dict(eig_slab=eig_slab, reflectors=reflectors, row_offsets=row_offsets)


def apply_sweep(eig_rows, eigen_columns, first_row, row_displacement, row_count_total, band_width):
    length, columns = eig_rows.shape
    overall_row_span = first_row + jnp.arange(length, dtype=jnp.int32)
    active_flags = (overall_row_span >= row_displacement) & (overall_row_span < row_count_total)
    eigen_columns = jnp.where(active_flags, eigen_columns, jnp.float32(0.0))
    shift = jnp.mod(row_displacement - first_row, band_width).astype(jnp.int32)
    zero_rows = jnp.zeros((band_width, columns), eig_rows.dtype)
    padded = jnp.concatenate([zero_rows, eig_rows, zero_rows], axis=0)
    zero_vec = jnp.zeros((band_width,), eigen_columns.dtype)
    padded_vec = jnp.concatenate([zero_vec, eigen_columns, zero_vec])
    integer_nought = jnp.zeros((band_width,), jnp.int32)
    extended_active_flags = jnp.concatenate([integer_nought, active_flags.astype(jnp.int32), integer_nought])
    windows_count = (length + band_width) // band_width
    windows = lax.dynamic_slice_in_dim(padded, shift, length + band_width, 0).reshape(windows_count, band_width, columns)
    window_vecs = lax.dynamic_slice_in_dim(padded_vec, shift, length + band_width, 0).reshape(windows_count, band_width)
    live_count = jnp.sum(lax.dynamic_slice_in_dim(extended_active_flags, shift, length + band_width, 0).reshape(windows_count, band_width), axis=1)
    squares = jnp.sum(window_vecs * window_vecs, axis=1)
    factor = jnp.where(live_count > 0, 2.0 / (squares + (live_count == 0).astype(jnp.float32)), jnp.float32(0.0))
    project = jnp.einsum("wr,wrc->wc", window_vecs, windows, precision=lax.Precision.HIGHEST)
    updated = windows - (factor[:, None] * window_vecs)[:, :, None] * project[:, None, :]
    padded = lax.dynamic_update_slice_in_dim(padded, updated.reshape(length + band_width, columns), shift, 0)
    return padded[band_width:band_width + length]


def reference(eig_slab, reflectors, row_offsets):
    col_block = math.gcd(NCOLS, 512)
    blocks = eig_slab.reshape(NROWS, NCOLS // col_block, col_block).transpose(1, 0, 2)

    def one_block(block_rows):
        for sweep_index in range(SWEEPS):
            block_rows = apply_sweep(block_rows, reflectors[sweep_index], 0, row_offsets[sweep_index], NROWS, WIDTH)
        return block_rows

    result = lax.map(one_block, blocks)
    return result.transpose(1, 0, 2).reshape(NROWS, NCOLS)
```

```python
import functools

import jax
import jax.numpy as jnp
from jax import lax
from jax.experimental import pallas as pl
from jax.experimental.pallas import tpu as pltpu
from jax.sharding import PartitionSpec as P

WIDTH = 64
SWEEPS = 16
RIM = 24
FRAME = WIDTH + RIM
EARLY = 16
LANES = 128
MESH = pl.DeviceIdType.MESH
HIGH = lax.Precision.HIGH
HIGHEST = lax.Precision.HIGHEST


def local_kernel(
    row_count, col_count,
    off_ref, refl_ref, x_ref,
    y_ref, inflow_ref,
    xe, vrec, vv, osend, orec, o2rec,
    x_sem, y_sem, send_sems, recv_sems, edge_send, edge_recv,
):
    per, rows = refl_ref.shape
    cols = x_ref.shape[1]
    wide = cols + LANES
    b = lax.axis_index("row")
    c = lax.axis_index("col")

    def row_at(d):
        return lax.rem(b + d + row_count, row_count)

    def col_at(d):
        return lax.rem(c + d, col_count)

    x_copy = pltpu.make_async_copy(x_ref, xe.at[WIDTH : WIDTH + rows, 0:cols], x_sem)
    x_copy.start()

    barrier = pltpu.get_barrier_semaphore()
    peers = [(b, col_at(d)) for d in range(1, col_count)]
    peers += [(row_at(e), col_at(d)) for e in (1, -1) for d in range(col_count)]
    peers += [(row_at(2), c), (row_at(-2), c)]
    for peer in peers:
        pl.semaphore_signal(barrier, inc=1, device_id=peer, device_id_type=MESH)

    xe[WIDTH + rows : WIDTH + rows + RIM, 0:cols] = jnp.zeros((RIM, cols), jnp.float32)
    xe[0 : WIDTH + rows, cols:wide] = jnp.zeros((WIDTH + rows, LANES), jnp.float32)
    unit = lax.broadcasted_iota(jnp.int32, (RIM, LANES), 0) == lax.broadcasted_iota(
        jnp.int32, (RIM, LANES), 1
    )
    xe[WIDTH + rows : WIDTH + rows + RIM, cols:wide] = jnp.where(unit, 1.0, 0.0)
    vrec[c, :, LANES : LANES + rows] = refl_ref[...]

    pl.semaphore_wait(barrier, len(peers))

    copies = []

    def send(src, dst, slot, sender, peer):
        copy = pltpu.make_async_remote_copy(
            src_ref=src, dst_ref=dst, send_sem=send_sems.at[slot], recv_sem=recv_sems.at[sender],
            device_id=peer, device_id_type=MESH,
        )
        copy.start()
        copies.append(copy)

    slot = 0
    for d in range(1, col_count):
        send(refl_ref, vrec.at[c, :, LANES : LANES + rows], slot, d, (b, col_at(d)))
        slot += 1
    for d in range(col_count):
        send(
            refl_ref.at[:, 0:LANES], vrec.at[c, :, LANES + rows : 2 * LANES + rows],
            slot, col_count + d, (row_at(-1), col_at(d)),
        )
        slot += 1
        send(
            refl_ref.at[:, rows - LANES : rows], vrec.at[c, :, 0:LANES],
            slot, 2 * col_count + d, (row_at(1), col_at(d)),
        )
        slot += 1
    halo = pltpu.make_async_remote_copy(
        src_ref=x_ref.at[rows - WIDTH : rows, :], dst_ref=xe.at[0:WIDTH, 0:cols],
        send_sem=edge_send.at[0], recv_sem=edge_recv.at[0],
        device_id=(row_at(1), c), device_id_type=MESH,
    )
    halo.start()

    for copy in copies:
        copy.wait_recv()

    for i in range(col_count):
        vv[i * per : (i + 1) * per, :] = vrec[i]

    sweep_of = lax.broadcasted_iota(jnp.int32, (SWEEPS, LANES), 0)
    lane_of = lax.broadcasted_iota(jnp.int32, (SWEEPS, LANES), 1)
    first = jnp.zeros((SWEEPS, LANES), jnp.int32)
    for s in range(SWEEPS):
        first = jnp.where(sweep_of == s, off_ref[s], first)
    window = (lane_of >= first) & (lane_of < first + WIDTH)

    vall = vv[...]
    turned = pltpu.roll(vall, vall.shape[1] - WIDTH, 1)
    count = rows // WIDTH + 1
    products = []
    for f in range(count):
        if f % 2 == 0:
            v = turned[:, WIDTH * f : WIDTH * f + LANES]
        else:
            v = vall[:, WIDTH * (f + 1) : WIDTH * (f + 1) + LANES]
        live = window
        if f == 0:
            live = live & (b > 0)
        if f == count - 1:
            live = live & ((lane_of < WIDTH) | (b < row_count - 1))
        v = jnp.where(live, v, 0.0)
        squares = jnp.sum(v * v, axis=1, keepdims=True)
        if f == 0:
            dead = (b == 0).astype(jnp.float32)
            tau = jnp.where(b > 0, 2.0 / (squares + dead), 0.0)
        else:
            tau = 2.0 / squares
        gram = lax.dot_general(
            v, v, (((1,), (1,)), ((), ())), precision=HIGHEST, preferred_element_type=jnp.float32
        )
        below = lax.broadcasted_iota(jnp.int32, (SWEEPS, SWEEPS), 0) > lax.broadcasted_iota(
            jnp.int32, (SWEEPS, SWEEPS), 1
        )
        scaled = jnp.where(below, gram * tau, 0.0)
        w = v * tau
        for j in range(SWEEPS - 1):
            w = w - scaled[:, j : j + 1] * w[j : j + 1, :]
        products.append(
            lax.dot_general(
                v, w, (((0,), (0,)), ((), ())), precision=HIGHEST, preferred_element_type=jnp.float32
            )
        )

    x_copy.wait()
    for f in range(count - 1, -1, -1):
        if f == 0:
            osend[...] = xe[WIDTH : WIDTH + RIM, :]
            far = pltpu.make_async_remote_copy(
                src_ref=osend.at[0:EARLY, 0:cols], dst_ref=o2rec,
                send_sem=edge_send.at[2], recv_sem=edge_recv.at[2],
                device_id=(row_at(-2), c), device_id_type=MESH,
            )
            near = pltpu.make_async_remote_copy(
                src_ref=osend, dst_ref=orec,
                send_sem=edge_send.at[1], recv_sem=edge_recv.at[1],
                device_id=(row_at(-1), c), device_id_type=MESH,
            )
            near.start()
            far.start()
            halo.wait_recv()
        frame = xe[WIDTH * f : WIDTH * f + FRAME, :]
        xe[WIDTH * f : WIDTH * f + FRAME, :] = frame - jnp.dot(
            products[f][0:FRAME, 0:FRAME], frame, precision=HIGH, preferred_element_type=jnp.float32
        )

    y_copy = pltpu.make_async_copy(xe.at[WIDTH : WIDTH + rows, :], y_ref, y_sem)
    y_copy.start()

    near.wait_recv()
    far.wait_recv()
    inflow_ref[0:8, :] = orec[0:8, 0:cols]
    inflow_ref[8:RIM, :] = orec[8:RIM, 0:cols] + jnp.dot(
        orec[8:RIM, cols : cols + EARLY], o2rec[...], precision=HIGH, preferred_element_type=jnp.float32
    )

    for copy in copies:
        copy.wait_send()
    halo.wait_send()
    near.wait_send()
    far.wait_send()
    y_copy.wait()


def finish_kernel(y_ref, inflow_ref, out_ref):
    cols = out_ref.shape[1]
    out_ref[...] = y_ref[:, 0:cols] + jnp.dot(
        y_ref[:, cols : cols + RIM], inflow_ref[...], precision=HIGH, preferred_element_type=jnp.float32
    )


def local(row_count, col_count, eig_slab, reflectors, row_offsets):
    rows, cols = eig_slab.shape
    per = reflectors.shape[0]
    wide = cols + LANES
    sends = 3 * col_count - 1
    y, inflow = pl.pallas_call(
        functools.partial(local_kernel, row_count, col_count),
        out_shape=(
            jax.ShapeDtypeStruct((rows, wide), jnp.float32),
            jax.ShapeDtypeStruct((RIM, cols), jnp.float32),
        ),
        in_specs=[
            pl.BlockSpec(memory_space=pltpu.SMEM),
            pl.BlockSpec(memory_space=pltpu.VMEM),
            pl.BlockSpec(memory_space=pl.ANY),
        ],
        out_specs=(pl.BlockSpec(memory_space=pl.ANY), pl.BlockSpec(memory_space=pltpu.VMEM)),
        scratch_shapes=[
            pltpu.VMEM((WIDTH + rows + RIM, wide), jnp.float32),
            pltpu.VMEM((col_count, per, rows + 2 * LANES), jnp.float32),
            pltpu.VMEM((SWEEPS, rows + 2 * LANES), jnp.float32),
            pltpu.VMEM((RIM, wide), jnp.float32),
            pltpu.VMEM((RIM, wide), jnp.float32),
            pltpu.VMEM((EARLY, cols), jnp.float32),
            pltpu.SemaphoreType.DMA,
            pltpu.SemaphoreType.DMA,
            pltpu.SemaphoreType.DMA((sends,)),
            pltpu.SemaphoreType.DMA((3 * col_count,)),
            pltpu.SemaphoreType.DMA((3,)),
            pltpu.SemaphoreType.DMA((3,)),
        ],
        compiler_params=pltpu.CompilerParams(
            collective_id=0, has_side_effects=True, vmem_limit_bytes=24 * 2**20
        ),
        name="sweep",
    )(row_offsets, reflectors, eig_slab)
    step = 128
    return pl.pallas_call(
        finish_kernel,
        out_shape=jax.ShapeDtypeStruct((rows, cols), jnp.float32),
        grid=(rows // step,),
        in_specs=[
            pl.BlockSpec((step, wide), lambda i: (i, 0)),
            pl.BlockSpec((RIM, cols), lambda i: (0, 0)),
        ],
        out_specs=pl.BlockSpec((step, cols), lambda i: (i, 0)),
        name="finish",
    )(y, inflow)


def solution(mesh):
    placed = (P("row", "col"), P("col", "row"), P())
    return jax.shard_map(
        functools.partial(local, mesh.shape["row"], mesh.shape["col"]),
        mesh=mesh, in_specs=placed, out_specs=P("row", "col"), check_vma=False,
    )
```

```python
import functools

import jax
import jax.numpy as jnp
from jax import lax
from jax.experimental import pallas as pl
from jax.experimental.pallas import tpu as pltpu
from jax.sharding import PartitionSpec as P

WIDTH = 64
SWEEPS = 16
RIM = 24
FRAME = WIDTH + RIM
EARLY = 16
LANES = 128
TURN = 16
MESH = pl.DeviceIdType.MESH
F32 = jnp.float32
HIGH = lax.Precision.HIGH
HIGHEST = lax.Precision.HIGHEST


def dot(a, b, precision=HIGH):
    return jnp.dot(a, b, precision=precision, preferred_element_type=F32)


def halves(x):
    head = x.astype(jnp.bfloat16)
    return head, (x - head.astype(F32)).astype(jnp.bfloat16)


def substituted(scaled, base, w):
    half = SWEEPS // 2
    top, bottom = w[0:half], w[half:SWEEPS]
    for j in range(SWEEPS - 1):
        column = slice(base + j, base + j + 1)
        if j < half:
            row = top[j : j + 1]
            if j < half - 1:
                top = top - scaled[0:half, column] * row
        else:
            row = bottom[j - half : j - half + 1]
        bottom = bottom - scaled[half:SWEEPS, column] * row
    return jnp.concatenate([top, bottom], axis=0)


def combined(frames, taus):
    v_all = jnp.concatenate(frames, axis=0)
    tau = jnp.concatenate(taus, axis=0)
    n = v_all.shape[0]
    gram = lax.dot_general(
        v_all, v_all, (((1,), (1,)), ((), ())), precision=HIGHEST, preferred_element_type=F32
    )
    scaled = gram * tau
    w_all = v_all * tau
    out = []
    for i, v in enumerate(frames):
        lo = SWEEPS * i
        block = scaled[lo : lo + SWEEPS, 0:n]
        below = lax.broadcasted_iota(jnp.int32, (SWEEPS, n), 0) > (
            lax.broadcasted_iota(jnp.int32, (SWEEPS, n), 1) - lo
        )
        block = jnp.where(below, block, 0.0)
        w = substituted(block, lo, w_all[lo : lo + SWEEPS])
        vh, vl = halves(v)
        wh, wl = halves(w)
        product = lax.dot_general(
            jnp.concatenate([vh, vh, vl], axis=0), jnp.concatenate([wh, wl, wh], axis=0),
            (((0,), (0,)), ((), ())), preferred_element_type=F32,
        )
        out.append((w, product))
    return out


def sweep_kernel(
    row_count, col_count,
    off_hbm, refl_hbm, x_hbm,
    y_ref,
    off_ref, xe, vrec, vv, heads, tails, osend, orec, o2rec, first_product,
    local_sems, send_sems, recv_sems, edge_send, edge_recv, ready,
):
    per, rows = refl_hbm.shape
    cols = x_hbm.shape[1]
    wide = cols + LANES
    chains = rows // WIDTH
    b = lax.axis_index("row")
    c = lax.axis_index("col")
    below1, below2 = (b - 1, c), (b - 2, c)
    above1, above2 = (b + 1, c), (b + 2, c)
    has_below1, has_below2 = b >= 1, b >= 2
    has_above1, has_above2 = b < row_count - 1, b < row_count - 2
    far1 = lax.rem(b, TURN) == 0
    far2 = lax.rem(b, TURN) < 2

    def col_at(d):
        return lax.rem(c + d, col_count)

    barrier = pltpu.get_barrier_semaphore()

    def greet(peer):
        pl.semaphore_signal(barrier, inc=1, device_id=peer, device_id_type=MESH)

    order = sorted(range(1, col_count), key=lambda d: -min(d, col_count - d))
    for d in order:
        greet((b, col_at(d)))
    pl.when(has_below1)(lambda: greet(below1))
    pl.when(has_below2)(lambda: greet(below2))

    refl_copy = pltpu.make_async_copy(refl_hbm, vrec.at[c], local_sems.at[0])
    off_copy = pltpu.make_async_copy(off_hbm, off_ref, local_sems.at[1])
    x_copy = pltpu.make_async_copy(x_hbm, xe.at[WIDTH : WIDTH + rows, 0:cols], local_sems.at[2])
    refl_copy.start()
    off_copy.start()
    x_copy.start()

    xe[WIDTH + rows : WIDTH + rows + RIM, 0:cols] = jnp.zeros((RIM, cols), F32)
    xe[WIDTH : WIDTH + rows, cols:wide] = jnp.zeros((rows, LANES), F32)
    unit = lax.broadcasted_iota(jnp.int32, (RIM, LANES), 0) == lax.broadcasted_iota(
        jnp.int32, (RIM, LANES), 1
    )
    unit = jnp.where(unit, 1.0, 0.0)
    xe[WIDTH + rows : WIDTH + rows + RIM, cols:wide] = unit

    @pl.when(b == 0)
    def _():
        xe[0:WIDTH, 0:cols] = jnp.zeros((WIDTH, cols), F32)

    @pl.when(b == row_count - 1)
    def _():
        orec[...] = jnp.zeros((RIM, wide), F32)

    @pl.when(b >= row_count - 2)
    def _():
        o2rec[...] = jnp.zeros((EARLY, cols), F32)

    pl.semaphore_wait(
        barrier, col_count - 1 + has_above1.astype(jnp.int32) + has_above2.astype(jnp.int32)
    )

    gathers = []
    for d in order:
        copy = pltpu.make_async_remote_copy(
            src_ref=refl_hbm, dst_ref=vrec.at[c], send_sem=send_sems.at[d], recv_sem=recv_sems.at[d],
            device_id=(b, col_at(d)), device_id_type=MESH,
        )
        copy.start()
        gathers.append(copy)

    def edge(i, src, dst, peer):
        return pltpu.make_async_remote_copy(
            src_ref=src, dst_ref=dst, send_sem=edge_send.at[i], recv_sem=edge_recv.at[i],
            device_id=peer, device_id_type=MESH,
        )

    halo_copy = edge(0, x_hbm.at[rows - WIDTH : rows, :], xe.at[0:WIDTH, 0:cols], above1)
    tails_copy = edge(1, vv.at[:, rows - LANES : rows], tails, above1)
    heads_copy = edge(2, vv.at[:, 0:LANES], heads, below1)
    near_copy = edge(3, osend, orec, below1)
    far_copy = edge(4, osend.at[0:EARLY, 0:cols], o2rec, below2)

    def tell(i, peer):
        pl.semaphore_signal(ready.at[i], inc=1, device_id=peer, device_id_type=MESH)

    @pl.when(has_above1)
    def _():
        tell(0, above1)
        halo_copy.start()

    pl.when(has_above2)(lambda: tell(1, above2))

    refl_copy.wait()
    off_copy.wait()
    for copy in gathers:
        copy.wait_recv()
    for i in range(col_count):
        vv[i * per : (i + 1) * per, :] = vrec[i]

    def send_heads():
        pl.semaphore_wait(ready.at[0], 1)
        heads_copy.start()

    pl.when(has_above1)(tails_copy.start)
    pl.when(has_below1 & jnp.logical_not(far1))(send_heads)

    sweep_of = lax.broadcasted_iota(jnp.int32, (SWEEPS, LANES), 0)
    lane_of = lax.broadcasted_iota(jnp.int32, (SWEEPS, LANES), 1)
    first = jnp.zeros((SWEEPS, LANES), jnp.int32)
    for s in range(SWEEPS):
        first = jnp.where(sweep_of == s, off_ref[s], first)
    window = (lane_of >= first) & (lane_of < first + WIDTH)

    own = vv[...]
    turned = pltpu.roll(own, rows - WIDTH, 1)
    frames = []
    for k in range(chains - 1):
        lo = WIDTH * k
        v = own[:, lo : lo + LANES] if k % 2 == 0 else turned[:, lo - WIDTH : lo - WIDTH + LANES]
        frames.append(jnp.where(window, v, 0.0))
    taus = [2.0 / jnp.sum(v * v, axis=1, keepdims=True) for v in frames]
    products = [product for _, product in combined(frames, taus)]

    x_copy.wait()
    form = unit - products[0][0:RIM]
    outflow = dot(form[:, 0:WIDTH], xe[WIDTH : 2 * WIDTH, 0:cols])
    for k in range(1, chains - 1):
        form = dot(form[:, WIDTH:FRAME], unit - products[k][0:RIM])
        outflow = outflow + dot(form[:, 0:WIDTH], xe[WIDTH * (k + 1) : WIDTH * (k + 2), 0:cols])
    onward = form[:, WIDTH:FRAME]

    pl.when(has_above1)(heads_copy.wait_recv)
    v = jnp.concatenate([own[:, rows - WIDTH : rows], heads[:, 0:WIDTH]], axis=1)
    v = jnp.where(window & ((lane_of < WIDTH) | has_above1), v, 0.0)
    tau = 2.0 / jnp.sum(v * v, axis=1, keepdims=True)
    ((_, product),) = combined([v], [tau])
    products.append(product)
    form = dot(onward, unit - product[0:RIM])
    osend[:, 0:cols] = outflow + dot(form[:, 0:WIDTH], xe[rows : rows + WIDTH, 0:cols])
    osend[:, cols:wide] = jnp.concatenate([form[:, WIDTH:LANES], jnp.zeros((RIM, WIDTH), F32)], axis=1)

    def send_far():
        pl.semaphore_wait(ready.at[1], 1)
        far_copy.start()

    pl.when(has_below1 & jnp.logical_not(far1))(near_copy.start)
    pl.when(has_below2 & jnp.logical_not(far2))(send_far)

    def lower_chain():
        pl.when(has_below1)(tails_copy.wait_recv)
        v = jnp.concatenate([tails[:, WIDTH:LANES], vv[:, 0:WIDTH]], axis=1)
        v = jnp.where(window & has_below1, v, 0.0)
        dead = jnp.where(has_below1, 0.0, 1.0)
        tau = jnp.where(has_below1, 2.0 / (jnp.sum(v * v, axis=1, keepdims=True) + dead), 0.0)
        ((_, product),) = combined([v], [tau])
        first_product[...] = product[WIDTH:FRAME]

    pl.when(jnp.logical_not(far1))(lower_chain)

    for k in range(chains - 1, -1, -1):
        lo = WIDTH * (k + 1)
        frame = xe[lo : lo + FRAME, :]
        xe[lo : lo + FRAME, :] = frame - dot(products[k][0:FRAME, 0:FRAME], frame)

    @pl.when(has_below1 & far1)
    def _():
        send_heads()
        near_copy.start()

    pl.when(has_below2 & far2)(send_far)

    pl.when(has_above1)(near_copy.wait_recv)
    pl.when(has_above2)(far_copy.wait_recv)
    early = RIM - EARLY
    inflow = jnp.concatenate(
        [
            orec[0:early, 0:cols],
            orec[early:RIM, 0:cols] + dot(orec[early:RIM, cols : cols + EARLY], o2rec[...]),
        ],
        axis=0,
    )
    y_ref[...] = xe[WIDTH : WIDTH + rows, 0:cols] + dot(
        xe[WIDTH : WIDTH + rows, cols : cols + RIM], inflow
    )

    pl.when(far1)(lower_chain)
    pl.when(has_below1)(halo_copy.wait_recv)
    frame = jnp.concatenate([xe[0:WIDTH, 0:cols], y_ref[0:RIM, :]], axis=0)
    y_ref[0:RIM, :] = y_ref[0:RIM, :] - dot(first_product[:, 0:FRAME], frame)

    for copy in gathers:
        copy.wait_send()

    @pl.when(has_above1)
    def _():
        halo_copy.wait_send()
        tails_copy.wait_send()

    @pl.when(has_below1)
    def _():
        heads_copy.wait_send()
        near_copy.wait_send()

    pl.when(has_below2)(far_copy.wait_send)


def local(row_count, col_count, eig_slab, reflectors, row_offsets):
    rows, cols = eig_slab.shape
    per = reflectors.shape[0]
    wide = cols + LANES
    return pl.pallas_call(
        functools.partial(sweep_kernel, row_count, col_count),
        out_shape=jax.ShapeDtypeStruct((rows, cols), F32),
        in_specs=[pl.BlockSpec(memory_space=pltpu.HBM)] * 3,
        out_specs=pl.BlockSpec(memory_space=pltpu.VMEM),
        scratch_shapes=[
            pltpu.SMEM((SWEEPS,), jnp.int32),
            pltpu.VMEM((WIDTH + rows + RIM, wide), F32),
            pltpu.VMEM((col_count, per, rows), F32),
            pltpu.VMEM((SWEEPS, rows), F32),
            pltpu.VMEM((SWEEPS, LANES), F32),
            pltpu.VMEM((SWEEPS, LANES), F32),
            pltpu.VMEM((RIM, wide), F32),
            pltpu.VMEM((RIM, wide), F32),
            pltpu.VMEM((EARLY, cols), F32),
            pltpu.VMEM((RIM, LANES), F32),
            pltpu.SemaphoreType.DMA((3,)),
            pltpu.SemaphoreType.DMA((col_count,)),
            pltpu.SemaphoreType.DMA((col_count,)),
            pltpu.SemaphoreType.DMA((5,)),
            pltpu.SemaphoreType.DMA((5,)),
            pltpu.SemaphoreType.REGULAR((2,)),
        ],
        compiler_params=pltpu.CompilerParams(
            collective_id=0, has_side_effects=True, vmem_limit_bytes=24 * 2**20
        ),
        name="sweep",
    )(*(pltpu.with_memory_space_constraint(a, pltpu.HBM) for a in (row_offsets, reflectors, eig_slab)))


def solution(mesh):
    placed = (P("row", "col"), P("col", "row"), P())
    return jax.shard_map(
        functools.partial(local, mesh.shape["row"], mesh.shape["col"]),
        mesh=mesh, in_specs=placed, out_specs=P("row", "col"), check_vma=False,
    )
```

```python
import functools

import jax
import jax.numpy as jnp
from jax import lax
from jax.experimental import pallas as pl
from jax.experimental.pallas import tpu as pltpu
from jax.sharding import PartitionSpec as P

WIDTH = 64
SWEEPS = 16
RIM = 24
FRAME = WIDTH + RIM
EARLY = 16
LANES = 128
TURN = 16
MESH = pl.DeviceIdType.MESH
F32 = jnp.float32
HIGH = lax.Precision.HIGH
HIGHEST = lax.Precision.HIGHEST


def dot(a, b, precision=HIGH):
    return jnp.dot(a, b, precision=precision, preferred_element_type=F32)


def halves(x):
    head = x.astype(jnp.bfloat16)
    return head, (x - head.astype(F32)).astype(jnp.bfloat16)


def substituted(scaled, base, w):
    half = SWEEPS // 2
    top, bottom = w[0:half], w[half:SWEEPS]
    for j in range(SWEEPS - 1):
        column = slice(base + j, base + j + 1)
        if j < half:
            row = top[j : j + 1]
            if j < half - 1:
                top = top - scaled[0:half, column] * row
        else:
            row = bottom[j - half : j - half + 1]
        bottom = bottom - scaled[half:SWEEPS, column] * row
    return jnp.concatenate([top, bottom], axis=0)


def combined(frames, taus):
    v_all = jnp.concatenate(frames, axis=0)
    tau = jnp.concatenate(taus, axis=0)
    n = v_all.shape[0]
    gram = lax.dot_general(
        v_all, v_all, (((1,), (1,)), ((), ())), precision=HIGHEST, preferred_element_type=F32
    )
    scaled = gram * tau
    w_all = v_all * tau
    out = []
    for i, v in enumerate(frames):
        lo = SWEEPS * i
        block = scaled[lo : lo + SWEEPS, 0:n]
        below = lax.broadcasted_iota(jnp.int32, (SWEEPS, n), 0) > (
            lax.broadcasted_iota(jnp.int32, (SWEEPS, n), 1) - lo
        )
        block = jnp.where(below, block, 0.0)
        w = substituted(block, lo, w_all[lo : lo + SWEEPS])
        vh, vl = halves(v)
        wh, wl = halves(w)
        product = lax.dot_general(
            jnp.concatenate([vh, vh, vl], axis=0), jnp.concatenate([wh, wl, wh], axis=0),
            (((0,), (0,)), ((), ())), preferred_element_type=F32,
        )
        out.append((w, product))
    return out


def sweep_kernel(
    row_count, col_count,
    off_hbm, refl_hbm, x_hbm,
    y_ref,
    off_ref, xe, vrec, vv, heads, tails, osend, fsend, orec, o2rec, first_product,
    local_sems, send_sems, recv_sems, edge_send, edge_recv, ready,
):
    per, rows = refl_hbm.shape
    cols = x_hbm.shape[1]
    wide = cols + LANES
    chains = rows // WIDTH
    b = lax.axis_index("row")
    c = lax.axis_index("col")
    below1, below2 = (b - 1, c), (b - 2, c)
    above1, above2 = (b + 1, c), (b + 2, c)
    has_below1, has_below2 = b >= 1, b >= 2
    has_above1, has_above2 = b < row_count - 1, b < row_count - 2
    place = lax.rem(b, TURN)
    late_below1, late_below2 = has_below1 & (place == 0), has_below2 & (place < 2)
    late_above1, late_above2 = has_above1 & (place < TURN - 1), has_above2 & (place < TURN - 2)
    soon_below1, soon_below2 = has_below1 & (place > 0), has_below2 & (place > 1)
    soon_above1, soon_above2 = has_above1 & (place == TURN - 1), has_above2 & (place >= TURN - 2)
    neighbours = (
        (above1, late_above1, soon_above1, 0),
        (above2, late_above2, soon_above2, 1),
        (below1, late_below1, soon_below1, 2),
        (below2, late_below2, soon_below2, 3),
    )

    def col_at(d):
        return lax.rem(c + d, col_count)

    barrier = pltpu.get_barrier_semaphore()

    def greet(peer):
        pl.semaphore_signal(barrier, inc=1, device_id=peer, device_id_type=MESH)

    order = sorted(range(1, col_count), key=lambda d: -min(d, col_count - d))
    for d in order:
        greet((b, col_at(d)))
    for peer, late, _, _ in neighbours:
        pl.when(late)(functools.partial(greet, peer))

    refl_copy = pltpu.make_async_copy(refl_hbm, vrec.at[c], local_sems.at[0])
    off_copy = pltpu.make_async_copy(off_hbm, off_ref, local_sems.at[1])
    x_copy = pltpu.make_async_copy(x_hbm, xe.at[WIDTH : WIDTH + rows, 0:cols], local_sems.at[2])
    refl_copy.start()
    off_copy.start()
    x_copy.start()

    xe[WIDTH + rows : WIDTH + rows + RIM, 0:cols] = jnp.zeros((RIM, cols), F32)
    xe[WIDTH : WIDTH + rows, cols:wide] = jnp.zeros((rows, LANES), F32)
    unit = lax.broadcasted_iota(jnp.int32, (RIM, LANES), 0) == lax.broadcasted_iota(
        jnp.int32, (RIM, LANES), 1
    )
    unit = jnp.where(unit, 1.0, 0.0)
    xe[WIDTH + rows : WIDTH + rows + RIM, cols:wide] = unit

    @pl.when(b == 0)
    def _():
        xe[0:WIDTH, 0:cols] = jnp.zeros((WIDTH, cols), F32)

    @pl.when(b == row_count - 1)
    def _():
        orec[...] = jnp.zeros((RIM, wide), F32)

    @pl.when(b >= row_count - 2)
    def _():
        o2rec[...] = jnp.zeros((EARLY, cols), F32)

    greeted = col_count - 1
    for _, _, soon, _ in neighbours:
        greeted = greeted + soon.astype(jnp.int32)
    pl.semaphore_wait(barrier, greeted)

    gathers = []
    for d in order:
        copy = pltpu.make_async_remote_copy(
            src_ref=refl_hbm, dst_ref=vrec.at[c], send_sem=send_sems.at[d], recv_sem=recv_sems.at[d],
            device_id=(b, col_at(d)), device_id_type=MESH,
        )
        copy.start()
        gathers.append(copy)

    def edge(i, src, dst, peer):
        return pltpu.make_async_remote_copy(
            src_ref=src, dst_ref=dst, send_sem=edge_send.at[i], recv_sem=edge_recv.at[i],
            device_id=peer, device_id_type=MESH,
        )

    halo_copy = edge(0, x_hbm.at[rows - WIDTH : rows, :], xe.at[0:WIDTH, 0:cols], above1)
    tails_copy = edge(1, vv.at[:, rows - LANES : rows], tails, above1)
    heads_copy = edge(2, vv.at[:, 0:LANES], heads, below1)
    near_copy = edge(3, osend, orec, below1)
    far_copy = edge(4, fsend, o2rec, below2)

    def tell(i, peer):
        pl.semaphore_signal(ready.at[i], inc=1, device_id=peer, device_id_type=MESH)

    for peer, _, soon, i in neighbours:
        pl.when(soon)(functools.partial(tell, (i + 2) % 4, peer))

    def heard(i):
        pl.semaphore_wait(ready.at[i], 1)

    refl_copy.wait()
    off_copy.wait()
    for copy in gathers:
        copy.wait_recv()
    for i in range(col_count):
        vv[i * per : (i + 1) * per, :] = vrec[i]

    pl.when(soon_below1)(heads_copy.start)

    @pl.when(soon_above1)
    def _():
        tails_copy.start()
        halo_copy.start()

    sweep_of = lax.broadcasted_iota(jnp.int32, (SWEEPS, LANES), 0)
    lane_of = lax.broadcasted_iota(jnp.int32, (SWEEPS, LANES), 1)
    first = jnp.zeros((SWEEPS, LANES), jnp.int32)
    for s in range(SWEEPS):
        first = jnp.where(sweep_of == s, off_ref[s], first)
    window = (lane_of >= first) & (lane_of < first + WIDTH)

    own = vv[...]
    turned = pltpu.roll(own, rows - WIDTH, 1)
    frames = []
    for k in range(chains - 1):
        lo = WIDTH * k
        v = own[:, lo : lo + LANES] if k % 2 == 0 else turned[:, lo - WIDTH : lo - WIDTH + LANES]
        frames.append(jnp.where(window, v, 0.0))
    taus = [2.0 / jnp.sum(v * v, axis=1, keepdims=True) for v in frames]
    products = [product for _, product in combined(frames, taus)]

    x_copy.wait()
    form = unit - products[0][0:RIM]
    outflow = dot(form[:, 0:WIDTH], xe[WIDTH : 2 * WIDTH, 0:cols])
    for k in range(1, chains - 1):
        form = dot(form[:, WIDTH:FRAME], unit - products[k][0:RIM])
        outflow = outflow + dot(form[:, 0:WIDTH], xe[WIDTH * (k + 1) : WIDTH * (k + 2), 0:cols])
    onward = form[:, WIDTH:FRAME]

    fsend[...] = outflow[0:EARLY] + dot(onward[0:EARLY], xe[rows : rows + RIM, 0:cols])
    pl.when(soon_below2)(far_copy.start)

    @pl.when(late_above1)
    def _():
        heard(0)
        tails_copy.start()
        halo_copy.start()

    pl.when(late_above2)(lambda: heard(1))

    pl.when(has_above1)(heads_copy.wait_recv)
    v = jnp.concatenate([own[:, rows - WIDTH : rows], heads[:, 0:WIDTH]], axis=1)
    v = jnp.where(window & ((lane_of < WIDTH) | has_above1), v, 0.0)
    tau = 2.0 / jnp.sum(v * v, axis=1, keepdims=True)
    ((_, product),) = combined([v], [tau])
    products.append(product)
    form = dot(onward, unit - product[0:RIM])
    osend[:, 0:cols] = outflow + dot(form[:, 0:WIDTH], xe[rows : rows + WIDTH, 0:cols])
    osend[:, cols:wide] = jnp.concatenate([form[:, WIDTH:LANES], jnp.zeros((RIM, WIDTH), F32)], axis=1)

    pl.when(soon_below1)(near_copy.start)

    def lower_chain():
        pl.when(has_below1)(tails_copy.wait_recv)
        v = jnp.concatenate([tails[:, WIDTH:LANES], vv[:, 0:WIDTH]], axis=1)
        v = jnp.where(window & has_below1, v, 0.0)
        dead = jnp.where(has_below1, 0.0, 1.0)
        tau = jnp.where(has_below1, 2.0 / (jnp.sum(v * v, axis=1, keepdims=True) + dead), 0.0)
        ((_, product),) = combined([v], [tau])
        first_product[...] = product[WIDTH:FRAME]

    pl.when(place > 0)(lower_chain)

    for k in range(chains - 1, -1, -1):
        lo = WIDTH * (k + 1)
        frame = xe[lo : lo + FRAME, :]
        xe[lo : lo + FRAME, :] = frame - dot(products[k][0:FRAME, 0:FRAME], frame)

    @pl.when(late_below1)
    def _():
        heard(2)
        heads_copy.start()
        near_copy.start()

    @pl.when(late_below2)
    def _():
        heard(3)
        far_copy.start()

    pl.when(has_above1)(near_copy.wait_recv)
    pl.when(has_above2)(far_copy.wait_recv)
    early = RIM - EARLY
    inflow = jnp.concatenate(
        [
            orec[0:early, 0:cols],
            orec[early:RIM, 0:cols] + dot(orec[early:RIM, cols : cols + EARLY], o2rec[...]),
        ],
        axis=0,
    )
    y_ref[...] = xe[WIDTH : WIDTH + rows, 0:cols] + dot(
        xe[WIDTH : WIDTH + rows, cols : cols + RIM], inflow
    )

    pl.when(place == 0)(lower_chain)
    pl.when(has_below1)(halo_copy.wait_recv)
    frame = jnp.concatenate([xe[0:WIDTH, 0:cols], y_ref[0:RIM, :]], axis=0)
    y_ref[0:RIM, :] = y_ref[0:RIM, :] - dot(first_product[:, 0:FRAME], frame)

    for copy in gathers:
        copy.wait_send()

    @pl.when(has_above1)
    def _():
        halo_copy.wait_send()
        tails_copy.wait_send()

    @pl.when(has_below1)
    def _():
        heads_copy.wait_send()
        near_copy.wait_send()

    pl.when(has_below2)(far_copy.wait_send)


def local(row_count, col_count, eig_slab, reflectors, row_offsets):
    rows, cols = eig_slab.shape
    per = reflectors.shape[0]
    wide = cols + LANES
    return pl.pallas_call(
        functools.partial(sweep_kernel, row_count, col_count),
        out_shape=jax.ShapeDtypeStruct((rows, cols), F32),
        in_specs=[pl.BlockSpec(memory_space=pltpu.HBM)] * 3,
        out_specs=pl.BlockSpec(memory_space=pltpu.VMEM),
        scratch_shapes=[
            pltpu.SMEM((SWEEPS,), jnp.int32),
            pltpu.VMEM((WIDTH + rows + RIM, wide), F32),
            pltpu.VMEM((col_count, per, rows), F32),
            pltpu.VMEM((SWEEPS, rows), F32),
            pltpu.VMEM((SWEEPS, LANES), F32),
            pltpu.VMEM((SWEEPS, LANES), F32),
            pltpu.VMEM((RIM, wide), F32),
            pltpu.VMEM((EARLY, cols), F32),
            pltpu.VMEM((RIM, wide), F32),
            pltpu.VMEM((EARLY, cols), F32),
            pltpu.VMEM((RIM, LANES), F32),
            pltpu.SemaphoreType.DMA((3,)),
            pltpu.SemaphoreType.DMA((col_count,)),
            pltpu.SemaphoreType.DMA((col_count,)),
            pltpu.SemaphoreType.DMA((5,)),
            pltpu.SemaphoreType.DMA((5,)),
            pltpu.SemaphoreType.REGULAR((4,)),
        ],
        compiler_params=pltpu.CompilerParams(
            collective_id=0, has_side_effects=True, vmem_limit_bytes=24 * 2**20
        ),
        name="sweep",
    )(*(pltpu.with_memory_space_constraint(a, pltpu.HBM) for a in (row_offsets, reflectors, eig_slab)))


def solution(mesh):
    placed = (P("row", "col"), P("col", "row"), P())
    return jax.shard_map(
        functools.partial(local, mesh.shape["row"], mesh.shape["col"]),
        mesh=mesh, in_specs=placed, out_specs=P("row", "col"), check_vma=False,
    )
```

```python
import functools

import jax
import jax.numpy as jnp
from jax import lax
from jax.experimental import pallas as pl
from jax.experimental.pallas import tpu as pltpu
from jax.sharding import PartitionSpec as P

WIDTH = 64
SWEEPS = 16
RIM = 24
FRAME = WIDTH + RIM
EARLY = 16
LANES = 128
TURN = 16
MESH = pl.DeviceIdType.MESH
F32 = jnp.float32
HIGH = lax.Precision.HIGH
HIGHEST = lax.Precision.HIGHEST


def dot(a, b, precision=HIGH):
    return jnp.dot(a, b, precision=precision, preferred_element_type=F32)


def halves(x):
    head = x.astype(jnp.bfloat16)
    return head, (x - head.astype(F32)).astype(jnp.bfloat16)


def substituted(scaled, base, w):
    half = SWEEPS // 2
    top, bottom = w[0:half], w[half:SWEEPS]
    for j in range(SWEEPS - 1):
        column = slice(base + j, base + j + 1)
        if j < half:
            row = top[j : j + 1]
            if j < half - 1:
                top = top - scaled[0:half, column] * row
        else:
            row = bottom[j - half : j - half + 1]
        bottom = bottom - scaled[half:SWEEPS, column] * row
    return jnp.concatenate([top, bottom], axis=0)


def combined(frames, taus):
    v_all = jnp.concatenate(frames, axis=0)
    tau = jnp.concatenate(taus, axis=0)
    n = v_all.shape[0]
    gram = lax.dot_general(
        v_all, v_all, (((1,), (1,)), ((), ())), precision=HIGHEST, preferred_element_type=F32
    )
    scaled = gram * tau
    w_all = v_all * tau
    out = []
    for i, v in enumerate(frames):
        lo = SWEEPS * i
        block = scaled[lo : lo + SWEEPS, 0:n]
        below = lax.broadcasted_iota(jnp.int32, (SWEEPS, n), 0) > (
            lax.broadcasted_iota(jnp.int32, (SWEEPS, n), 1) - lo
        )
        block = jnp.where(below, block, 0.0)
        w = substituted(block, lo, w_all[lo : lo + SWEEPS])
        vh, vl = halves(v)
        wh, wl = halves(w)
        product = lax.dot_general(
            jnp.concatenate([vh, vh, vl], axis=0), jnp.concatenate([wh, wl, wh], axis=0),
            (((0,), (0,)), ((), ())), preferred_element_type=F32,
        )
        out.append((w, product))
    return out


def sweep_kernel(
    row_count, col_count,
    off_hbm, refl_hbm, x_hbm,
    y_ref,
    off_ref, xe, vrec, vv, heads, tails, tv, osend, fsend, orec, o2rec, first_product,
    local_sems, send_sems, recv_sems, tail_send, tail_recv, edge_send, edge_recv, ready,
):
    per, rows = refl_hbm.shape
    cols = x_hbm.shape[1]
    wide = cols + LANES
    chains = rows // WIDTH
    b = lax.axis_index("row")
    c = lax.axis_index("col")
    below1, below2 = (b - 1, c), (b - 2, c)
    above1, above2 = (b + 1, c), (b + 2, c)
    has_below1, has_below2 = b >= 1, b >= 2
    has_above1, has_above2 = b < row_count - 1, b < row_count - 2
    place = lax.rem(b, TURN)
    late_below1 = has_below1 & ((place == 0) | (b == 1))
    late_below2 = has_below2 & ((place < 2) | (b == 2))
    late_above1 = has_above1 & (place < TURN - 1) & (b > 0)
    late_above2 = has_above2 & (place < TURN - 2) & (b > 0)
    soon_below1, soon_below2 = has_below1 & jnp.logical_not(late_below1), has_below2 & jnp.logical_not(late_below2)
    soon_above1, soon_above2 = has_above1 & jnp.logical_not(late_above1), has_above2 & jnp.logical_not(late_above2)
    last_below1, last_below2 = late_below1 & (place == 0), late_below2 & (place < 2)
    next_below1, next_below2 = late_below1 & (place > 0), late_below2 & (place > 1)
    lower_last = (place == 0) | (b == 1)
    wide_above1 = soon_above1 & (place == TURN - 1)
    neighbours = (
        (above1, late_above1, soon_above1, 0),
        (above2, late_above2, soon_above2, 1),
        (below1, late_below1, soon_below1, 2),
        (below2, late_below2, soon_below2, 3),
    )

    barrier = pltpu.get_barrier_semaphore()

    def greet(peer):
        pl.semaphore_signal(barrier, inc=1, device_id=peer, device_id_type=MESH)

    def col_at(d):
        return lax.rem(c + d, col_count)

    order = sorted(range(1, col_count), key=lambda d: -min(d, col_count - d))
    for d in order:
        greet((b, col_at(d)))
    for i, (peer, late, _, _) in enumerate(neighbours):
        if i == 2:
            late = next_below1
        pl.when(late)(functools.partial(greet, peer))

    @pl.when(last_below1)
    def _():
        for d in range(col_count):
            greet((b - 1, col_at(d)))

    refl_copy = pltpu.make_async_copy(refl_hbm, vrec.at[c], local_sems.at[0])
    off_copy = pltpu.make_async_copy(off_hbm, off_ref, local_sems.at[1])
    x_copy = pltpu.make_async_copy(x_hbm, xe.at[WIDTH : WIDTH + rows, 0:cols], local_sems.at[2])
    refl_copy.start()
    off_copy.start()
    x_copy.start()

    xe[WIDTH + rows : WIDTH + rows + RIM, 0:cols] = jnp.zeros((RIM, cols), F32)
    xe[WIDTH : WIDTH + rows, cols:wide] = jnp.zeros((rows, LANES), F32)
    unit = lax.broadcasted_iota(jnp.int32, (RIM, LANES), 0) == lax.broadcasted_iota(
        jnp.int32, (RIM, LANES), 1
    )
    unit = jnp.where(unit, 1.0, 0.0)
    xe[WIDTH + rows : WIDTH + rows + RIM, cols:wide] = unit

    @pl.when(b == 0)
    def _():
        xe[0:WIDTH, 0:cols] = jnp.zeros((WIDTH, cols), F32)

    @pl.when(b == row_count - 1)
    def _():
        orec[...] = jnp.zeros((RIM, wide), F32)

    @pl.when(b >= row_count - 2)
    def _():
        o2rec[...] = jnp.zeros((EARLY, cols), F32)

    greeted = jnp.where(wide_above1, 2 * (col_count - 1), col_count - 1)
    for _, _, soon, _ in neighbours:
        greeted = greeted + soon.astype(jnp.int32)
    pl.semaphore_wait(barrier, greeted)

    refl_copy.wait()
    gathers = [
        pltpu.make_async_remote_copy(
            src_ref=vrec.at[c], dst_ref=vrec.at[c], send_sem=send_sems.at[d], recv_sem=recv_sems.at[d],
            device_id=(b, col_at(d)), device_id_type=MESH,
        )
        for d in order
    ]
    for copy in gathers:
        copy.start()

    def edge(i, src, dst, peer):
        return pltpu.make_async_remote_copy(
            src_ref=src, dst_ref=dst, send_sem=edge_send.at[i], recv_sem=edge_recv.at[i],
            device_id=peer, device_id_type=MESH,
        )

    halo_copy = edge(0, x_hbm.at[rows - WIDTH : rows, :], xe.at[0:WIDTH, 0:cols], above1)
    tails_copy = edge(1, vrec.at[:, :, rows - LANES : rows], tails, above1)
    tail_copies = [
        pltpu.make_async_remote_copy(
            src_ref=vrec.at[c, :, rows - LANES : rows], dst_ref=tails.at[c],
            send_sem=tail_send.at[d], recv_sem=tail_recv.at[d],
            device_id=(b + 1, col_at(d)), device_id_type=MESH,
        )
        for d in range(col_count)
    ]
    heads_copy = edge(2, vv.at[:, 0:LANES], heads, below1)
    near_copy = edge(3, osend, orec, below1)
    far_copy = edge(4, fsend, o2rec, below2)

    def tell(i, peer):
        pl.semaphore_signal(ready.at[i], inc=1, device_id=peer, device_id_type=MESH)

    for peer, _, soon, i in neighbours:
        pl.when(soon)(functools.partial(tell, (i + 2) % 4, peer))

    def heard(i):
        pl.semaphore_wait(ready.at[i], 1)

    @pl.when(wide_above1)
    def _():
        for copy in tail_copies:
            copy.start()

    pl.when(soon_above1)(halo_copy.start)


    off_copy.wait()
    for copy in gathers:
        copy.wait_recv()
    for i in range(col_count):
        vv[i * per : (i + 1) * per, :] = vrec[i]

    pl.when(soon_below1)(heads_copy.start)

    pl.when(soon_above1 & jnp.logical_not(wide_above1))(tails_copy.start)

    sweep_of = lax.broadcasted_iota(jnp.int32, (SWEEPS, LANES), 0)
    lane_of = lax.broadcasted_iota(jnp.int32, (SWEEPS, LANES), 1)
    first = jnp.zeros((SWEEPS, LANES), jnp.int32)
    for s in range(SWEEPS):
        first = jnp.where(sweep_of == s, off_ref[s], first)
    window = (lane_of >= first) & (lane_of < first + WIDTH)

    own = vv[...]
    turned = pltpu.roll(own, rows - WIDTH, 1)
    frames = []
    for k in range(chains - 1):
        lo = WIDTH * k
        v = own[:, lo : lo + LANES] if k % 2 == 0 else turned[:, lo - WIDTH : lo - WIDTH + LANES]
        frames.append(jnp.where(window, v, 0.0))
    taus = [2.0 / jnp.sum(v * v, axis=1, keepdims=True) for v in frames]
    products = [product for _, product in combined(frames, taus)]

    @pl.when(late_above1)
    def _():
        heard(0)
        tails_copy.start()
        halo_copy.start()

    pl.when(late_above2)(lambda: heard(1))

    @pl.when(next_below1)
    def _():
        heard(2)
        heads_copy.start()

    x_copy.wait()
    form = unit - products[0][0:RIM]
    outflow = dot(form[:, 0:WIDTH], xe[WIDTH : 2 * WIDTH, 0:cols])
    for k in range(1, chains - 1):
        form = dot(form[:, WIDTH:FRAME], unit - products[k][0:RIM])
        outflow = outflow + dot(form[:, 0:WIDTH], xe[WIDTH * (k + 1) : WIDTH * (k + 2), 0:cols])
    onward = form[:, WIDTH:FRAME]

    fsend[...] = outflow[0:EARLY] + dot(onward[0:EARLY], xe[rows : rows + RIM, 0:cols])
    pl.when(next_below2)(lambda: heard(3))
    pl.when(soon_below2 | next_below2)(far_copy.start)

    pl.when(has_above1)(heads_copy.wait_recv)
    v = jnp.concatenate([own[:, rows - WIDTH : rows], heads[:, 0:WIDTH]], axis=1)
    v = jnp.where(window & ((lane_of < WIDTH) | has_above1), v, 0.0)
    tau = 2.0 / jnp.sum(v * v, axis=1, keepdims=True)
    ((_, product),) = combined([v], [tau])
    products.append(product)
    form = dot(onward, unit - product[0:RIM])
    osend[:, 0:cols] = outflow + dot(form[:, 0:WIDTH], xe[rows : rows + WIDTH, 0:cols])
    osend[:, cols:wide] = jnp.concatenate([form[:, WIDTH:LANES], jnp.zeros((RIM, WIDTH), F32)], axis=1)

    pl.when(soon_below1 | next_below1)(near_copy.start)

    def lower_chain():
        pl.when(has_below1 & jnp.logical_not(last_below1))(tails_copy.wait_recv)

        @pl.when(last_below1)
        def _():
            for copy in tail_copies:
                copy.wait_recv()

        for i in range(col_count):
            tv[i * per : (i + 1) * per, :] = tails[i]
        v = jnp.concatenate([tv[:, WIDTH:LANES], vv[:, 0:WIDTH]], axis=1)
        v = jnp.where(window & has_below1, v, 0.0)
        dead = jnp.where(has_below1, 0.0, 1.0)
        tau = jnp.where(has_below1, 2.0 / (jnp.sum(v * v, axis=1, keepdims=True) + dead), 0.0)
        ((_, product),) = combined([v], [tau])
        first_product[...] = product[WIDTH:FRAME]


    for k in range(chains - 1, -1, -1):
        lo = WIDTH * (k + 1)
        frame = xe[lo : lo + FRAME, :]
        xe[lo : lo + FRAME, :] = frame - dot(products[k][0:FRAME, 0:FRAME], frame)

    pl.when(jnp.logical_not(lower_last))(lower_chain)

    @pl.when(last_below1)
    def _():
        heard(2)
        heads_copy.start()
        near_copy.start()

    @pl.when(last_below2)
    def _():
        heard(3)
        far_copy.start()

    pl.when(has_above1)(near_copy.wait_recv)
    pl.when(has_above2)(far_copy.wait_recv)
    early = RIM - EARLY
    inflow = jnp.concatenate(
        [
            orec[0:early, 0:cols],
            orec[early:RIM, 0:cols] + dot(orec[early:RIM, cols : cols + EARLY], o2rec[...]),
        ],
        axis=0,
    )
    y_ref[...] = xe[WIDTH : WIDTH + rows, 0:cols] + dot(
        xe[WIDTH : WIDTH + rows, cols : cols + RIM], inflow
    )

    pl.when(lower_last)(lower_chain)
    pl.when(has_below1)(halo_copy.wait_recv)
    frame = jnp.concatenate([xe[0:WIDTH, 0:cols], y_ref[0:RIM, :]], axis=0)
    y_ref[0:RIM, :] = y_ref[0:RIM, :] - dot(first_product[:, 0:FRAME], frame)

    for copy in gathers:
        copy.wait_send()

    pl.when(has_above1)(halo_copy.wait_send)
    pl.when(has_above1 & jnp.logical_not(wide_above1))(tails_copy.wait_send)

    @pl.when(wide_above1)
    def _():
        for copy in tail_copies:
            copy.wait_send()

    @pl.when(has_below1)
    def _():
        heads_copy.wait_send()
        near_copy.wait_send()

    pl.when(has_below2)(far_copy.wait_send)


def local(row_count, col_count, eig_slab, reflectors, row_offsets):
    rows, cols = eig_slab.shape
    per = reflectors.shape[0]
    wide = cols + LANES
    return pl.pallas_call(
        functools.partial(sweep_kernel, row_count, col_count),
        out_shape=jax.ShapeDtypeStruct((rows, cols), F32),
        in_specs=[pl.BlockSpec(memory_space=pltpu.HBM)] * 3,
        out_specs=pl.BlockSpec(memory_space=pltpu.VMEM),
        scratch_shapes=[
            pltpu.SMEM((SWEEPS,), jnp.int32),
            pltpu.VMEM((WIDTH + rows + RIM, wide), F32),
            pltpu.VMEM((col_count, per, rows), F32),
            pltpu.VMEM((SWEEPS, rows), F32),
            pltpu.VMEM((SWEEPS, LANES), F32),
            pltpu.VMEM((col_count, per, LANES), F32),
            pltpu.VMEM((SWEEPS, LANES), F32),
            pltpu.VMEM((RIM, wide), F32),
            pltpu.VMEM((EARLY, cols), F32),
            pltpu.VMEM((RIM, wide), F32),
            pltpu.VMEM((EARLY, cols), F32),
            pltpu.VMEM((RIM, LANES), F32),
            pltpu.SemaphoreType.DMA((3,)),
            pltpu.SemaphoreType.DMA((col_count,)),
            pltpu.SemaphoreType.DMA((col_count,)),
            pltpu.SemaphoreType.DMA((col_count,)),
            pltpu.SemaphoreType.DMA((col_count,)),
            pltpu.SemaphoreType.DMA((5,)),
            pltpu.SemaphoreType.DMA((5,)),
            pltpu.SemaphoreType.REGULAR((4,)),
        ],
        compiler_params=pltpu.CompilerParams(
            collective_id=0, has_side_effects=True, vmem_limit_bytes=24 * 2**20
        ),
        name="sweep",
    )(*(pltpu.with_memory_space_constraint(a, pltpu.HBM) for a in (row_offsets, reflectors, eig_slab)))


def solution(mesh):
    placed = (P("row", "col"), P("col", "row"), P())
    return jax.shard_map(
        functools.partial(local, mesh.shape["row"], mesh.shape["col"]),
        mesh=mesh, in_specs=placed, out_specs=P("row", "col"), check_vma=False,
    )
```

```python
import functools

import jax
import jax.numpy as jnp
from jax import lax
from jax.experimental import pallas as pl
from jax.experimental.pallas import tpu as pltpu
from jax.sharding import PartitionSpec as P

WIDTH = 64
SWEEPS = 16
RIM = 24
FRAME = WIDTH + RIM
EARLY = 16
LANES = 128
SLOT = 32
TURN = 16
MESH = pl.DeviceIdType.MESH
F32 = jnp.float32
HIGH = lax.Precision.HIGH
HIGHEST = lax.Precision.HIGHEST


def dot(a, b, precision=HIGH):
    return jnp.dot(a, b, precision=precision, preferred_element_type=F32)


def halves(x):
    head = x.astype(jnp.bfloat16)
    return head, (x - head.astype(F32)).astype(jnp.bfloat16)


def substituted(scaled, base, w):
    half = SWEEPS // 2
    top, bottom = w[0:half], w[half:SWEEPS]
    for j in range(SWEEPS - 1):
        column = slice(base + j, base + j + 1)
        if j < half:
            row = top[j : j + 1]
            if j < half - 1:
                top = top - scaled[0:half, column] * row
        else:
            row = bottom[j - half : j - half + 1]
        bottom = bottom - scaled[half:SWEEPS, column] * row
    return jnp.concatenate([top, bottom], axis=0)


def combined(frames, taus):
    v_all = jnp.concatenate(frames, axis=0)
    tau = jnp.concatenate(taus, axis=0)
    n = v_all.shape[0]
    gram = lax.dot_general(
        v_all, v_all, (((1,), (1,)), ((), ())), precision=HIGHEST, preferred_element_type=F32
    )
    scaled = gram * tau
    w_all = v_all * tau
    out = []
    for i, v in enumerate(frames):
        lo = SWEEPS * i
        block = scaled[lo : lo + SWEEPS, 0:n]
        below = lax.broadcasted_iota(jnp.int32, (SWEEPS, n), 0) > (
            lax.broadcasted_iota(jnp.int32, (SWEEPS, n), 1) - lo
        )
        block = jnp.where(below, block, 0.0)
        w = substituted(block, lo, w_all[lo : lo + SWEEPS])
        vh, vl = halves(v)
        wh, wl = halves(w)
        product = lax.dot_general(
            jnp.concatenate([vh, vh, vl], axis=0), jnp.concatenate([wh, wl, wh], axis=0),
            (((0,), (0,)), ((), ())), preferred_element_type=F32,
        )
        out.append((w, product))
    return out


def paired(upper, lower):
    lanes = upper.shape[1]
    entry = lax.broadcasted_iota(jnp.int32, (RIM, lanes), 0) == lax.broadcasted_iota(
        jnp.int32, (RIM, lanes), 1
    )
    passed = jnp.where(entry, 1.0, 0.0) - upper[0:RIM]
    right = dot(lower[0:FRAME, WIDTH:FRAME], passed)
    right = jnp.concatenate([right[0:WIDTH], right[WIDTH:FRAME] + upper[0:RIM], upper[RIM:FRAME]], axis=0)
    left = jnp.concatenate([lower[0:FRAME, 0:WIDTH], jnp.zeros((WIDTH, WIDTH), F32)], axis=0)
    return jnp.concatenate([left, right[:, 0:FRAME]], axis=1)


def sweep_kernel(
    row_count, col_count,
    off_hbm, refl_hbm, x_hbm,
    y_ref,
    off_ref, xe, vrec, vv, heads, tails, tv, osend, fsend, orec, o2rec, first_product, upper, single, pairs, reply,
    local_sems, send_sems, recv_sems, tail_send, tail_recv, edge_send, edge_recv, ready,
):
    per, rows = refl_hbm.shape
    cols = x_hbm.shape[1]
    wide = cols + LANES
    chains = rows // WIDTH
    b = lax.axis_index("row")
    c = lax.axis_index("col")
    below1, below2 = (b - 1, c), (b - 2, c)
    above1, above2 = (b + 1, c), (b + 2, c)
    has_below1, has_below2 = b >= 1, b >= 2
    has_above1, has_above2 = b < row_count - 1, b < row_count - 2
    place = lax.rem(b, TURN)
    late_below1 = has_below1 & ((place == 0) | (b == 1))
    late_below2 = has_below2 & ((place < 2) | (b == 2))
    late_above1 = has_above1 & (place < TURN - 1) & (b > 0)
    late_above2 = has_above2 & (place < TURN - 2) & (b > 0)
    soon_below1, soon_below2 = has_below1 & jnp.logical_not(late_below1), has_below2 & jnp.logical_not(late_below2)
    soon_above1, soon_above2 = has_above1 & jnp.logical_not(late_above1), has_above2 & jnp.logical_not(late_above2)
    last_below1, last_below2 = late_below1 & (place == 0), late_below2 & (place < 2)
    next_below1, next_below2 = late_below1 & (place > 0), late_below2 & (place > 1)
    lower_last = (place == 0) | (b == 1)
    wide_above1 = soon_above1 & (place == TURN - 1)
    neighbours = (
        (above1, late_above1, soon_above1, 0),
        (above2, late_above2, soon_above2, 1),
        (below1, late_below1, soon_below1, 2),
        (below2, late_below2, soon_below2, 3),
    )

    barrier = pltpu.get_barrier_semaphore()

    def greet(peer):
        pl.semaphore_signal(barrier, inc=1, device_id=peer, device_id_type=MESH)

    def col_at(d):
        return lax.rem(c + d, col_count)

    order = sorted(range(1, col_count), key=lambda d: -min(d, col_count - d))
    for d in order:
        greet((b, col_at(d)))
    for i, (peer, late, _, _) in enumerate(neighbours):
        if i == 2:
            late = next_below1
        pl.when(late)(functools.partial(greet, peer))

    @pl.when(last_below1)
    def _():
        for d in range(col_count):
            greet((b - 1, col_at(d)))

    refl_copy = pltpu.make_async_copy(refl_hbm, vrec.at[c], local_sems.at[0])
    off_copy = pltpu.make_async_copy(off_hbm, off_ref, local_sems.at[1])
    x_copy = pltpu.make_async_copy(x_hbm, xe.at[WIDTH : WIDTH + rows, 0:cols], local_sems.at[2])
    refl_copy.start()
    off_copy.start()
    x_copy.start()

    xe[:, cols:wide] = jnp.zeros((WIDTH + rows, LANES), F32)
    unit = lax.broadcasted_iota(jnp.int32, (RIM, LANES), 0) == lax.broadcasted_iota(
        jnp.int32, (RIM, LANES), 1
    )
    rim = jnp.concatenate([jnp.zeros((RIM, cols), F32), jnp.where(unit, 1.0, 0.0)], axis=1)

    @pl.when(b == 0)
    def _():
        xe[0:WIDTH, 0:cols] = jnp.zeros((WIDTH, cols), F32)

    @pl.when(b == row_count - 1)
    def _():
        orec[...] = jnp.zeros((RIM, wide), F32)

    @pl.when(b >= row_count - 2)
    def _():
        o2rec[...] = jnp.zeros((EARLY, cols), F32)

    greeted = jnp.where(wide_above1, 2 * (col_count - 1), col_count - 1)
    for _, _, soon, _ in neighbours:
        greeted = greeted + soon.astype(jnp.int32)
    pl.semaphore_wait(barrier, greeted)

    refl_copy.wait()
    gathers = [
        pltpu.make_async_remote_copy(
            src_ref=vrec.at[c], dst_ref=vrec.at[c], send_sem=send_sems.at[d], recv_sem=recv_sems.at[d],
            device_id=(b, col_at(d)), device_id_type=MESH,
        )
        for d in order
    ]
    for copy in gathers:
        copy.start()

    def edge(i, src, dst, peer):
        return pltpu.make_async_remote_copy(
            src_ref=src, dst_ref=dst, send_sem=edge_send.at[i], recv_sem=edge_recv.at[i],
            device_id=peer, device_id_type=MESH,
        )

    halo_copy = edge(0, x_hbm.at[rows - WIDTH : rows, :], xe.at[0:WIDTH, 0:cols], above1)
    tails_copy = edge(1, vrec.at[:, :, rows - LANES : rows], tails, above1)
    tail_copies = [
        pltpu.make_async_remote_copy(
            src_ref=vrec.at[c, :, rows - LANES : rows], dst_ref=tails.at[c],
            send_sem=tail_send.at[d], recv_sem=tail_recv.at[d],
            device_id=(b + 1, col_at(d)), device_id_type=MESH,
        )
        for d in range(col_count)
    ]
    heads_copy = edge(2, vv.at[:, 0:LANES], heads, below1)
    near_copy = edge(3, osend, orec, below1)
    far_copy = edge(4, fsend, o2rec, below2)

    def tell(i, peer):
        pl.semaphore_signal(ready.at[i], inc=1, device_id=peer, device_id_type=MESH)

    for peer, _, soon, i in neighbours:
        if i != 3:
            pl.when(soon)(functools.partial(tell, (i + 2) % 4, peer))

    def heard(i):
        pl.semaphore_wait(ready.at[i], 1)

    @pl.when(wide_above1)
    def _():
        for copy in tail_copies:
            copy.start()

    pl.when(soon_above1)(halo_copy.start)


    off_copy.wait()
    for copy in gathers:
        copy.wait_recv()
    for i in range(col_count):
        vv[i * per : (i + 1) * per, :] = vrec[i]

    pl.when(soon_below1)(heads_copy.start)

    pl.when(soon_above1 & jnp.logical_not(wide_above1))(tails_copy.start)

    def send_up():
        heard(0)
        tails_copy.start()
        halo_copy.start()

    slow_above1 = late_above1 & (place == TURN // 2 - 1)
    pl.when(late_above1 & jnp.logical_not(slow_above1))(send_up)

    sweep_of = lax.broadcasted_iota(jnp.int32, (SWEEPS, LANES), 0)
    lane_of = lax.broadcasted_iota(jnp.int32, (SWEEPS, LANES), 1)
    first = jnp.zeros((SWEEPS, LANES), jnp.int32)
    for s in range(SWEEPS):
        first = jnp.where(sweep_of == s, off_ref[s], first)
    window = (lane_of >= first) & (lane_of < first + WIDTH)

    def inner_frames():
        own = vv[...]
        turned = pltpu.roll(own, rows - WIDTH, 1)
        frames = []
        for k in range(chains - 1):
            lo = WIDTH * k
            v = own[:, lo : lo + LANES] if k % 2 == 0 else turned[:, lo - WIDTH : lo - WIDTH + LANES]
            frames.append(jnp.where(window, v, 0.0))
        return frames, [2.0 / jnp.sum(v * v, axis=1, keepdims=True) for v in frames]

    def upper_frame():
        v = jnp.concatenate([vv[:, rows - WIDTH : rows], heads[:, 0:WIDTH]], axis=1)
        v = jnp.where(window & ((lane_of < WIDTH) | has_above1), v, 0.0)
        return v, 2.0 / jnp.sum(v * v, axis=1, keepdims=True)

    def keep(products):
        single[...] = products[chains - 2][0:FRAME]
        for i, k in enumerate(range(chains - 3, 0, -2)):
            pairs[i] = paired(products[k], products[k - 1])

    def run_upper(product):
        raw = xe[top : top + WIDTH, :]
        upper[...] = raw - dot(product[0:WIDTH, 0:FRAME], jnp.concatenate([raw, rim], axis=0))

    top = rows
    x_copy.wait()

    prompt = lax.rem(b, 2) == 0

    @pl.when(prompt)
    def _():
        pl.when(has_above1)(heads_copy.wait_recv)
        frames, taus = inner_frames()
        v, tau = upper_frame()
        products = [product for _, product in combined(frames + [v], taus + [tau])]
        keep(products)
        run_upper(products[chains - 1])

    @pl.when(jnp.logical_not(prompt))
    def _():
        keep([product for _, product in combined(*inner_frames())])

    @pl.when(next_below1)
    def _():
        heard(2)
        heads_copy.start()

    frame = jnp.concatenate([xe[top - WIDTH : top, :], rim], axis=0)
    frame = frame - dot(single[:, 0:FRAME], frame)
    xe[top - WIDTH : top, :] = frame[0:WIDTH]
    above = frame[WIDTH:FRAME]
    span = WIDTH + FRAME
    for i, k in enumerate(range(chains - 3, 0, -2)):
        lo = WIDTH * k
        frame = xe[lo : lo + span, :]
        xe[lo : lo + span, :] = frame - dot(pairs[i], frame)

    def send_far():
        pl.when(next_below2)(lambda: heard(3))
        pl.when(soon_below2 | next_below2)(far_copy.start)

    fsend[...] = xe[WIDTH : WIDTH + EARLY, 0:cols] + dot(
        xe[WIDTH : WIDTH + EARLY, cols : cols + RIM], xe[top : top + RIM, 0:cols]
    )

    send_far()

    @pl.when(jnp.logical_not(prompt))
    def _():
        pl.when(slow_above1)(send_up)
        pl.when(has_above1)(heads_copy.wait_recv)
        v, tau = upper_frame()
        ((_, product),) = combined([v], [tau])
        run_upper(product)

    flow = jnp.concatenate(
        [xe[WIDTH : WIDTH + RIM, 0:cols], jnp.zeros((RIM, LANES), F32)], axis=1
    ) + dot(xe[WIDTH : WIDTH + RIM, cols : cols + RIM], upper[0:RIM, :])
    osend[...] = flow
    pl.when(soon_below1 | next_below1)(near_copy.start)

    carried = jnp.concatenate([xe[WIDTH + RIM : top, :], above], axis=0)
    xe[WIDTH : WIDTH + RIM, :] = flow
    moved = dot(carried[:, cols : cols + RIM], upper[0:RIM, :])
    xe[WIDTH + RIM : top + RIM, 0:cols] = carried[:, 0:cols] + moved[:, 0:cols]
    xe[WIDTH + RIM : top + RIM, cols:wide] = moved[:, cols:wide]
    xe[top + RIM : top + WIDTH, :] = upper[RIM:WIDTH, :]

    def lower_chain():
        pl.when(has_below1 & jnp.logical_not(last_below1))(tails_copy.wait_recv)

        @pl.when(last_below1)
        def _():
            for copy in tail_copies:
                copy.wait_recv()

        for i in range(col_count):
            tv[i * per : (i + 1) * per, :] = tails[i]
        v = jnp.concatenate([tv[:, WIDTH:LANES], vv[:, 0:WIDTH]], axis=1)
        v = jnp.where(window & has_below1, v, 0.0)
        dead = jnp.where(has_below1, 0.0, 1.0)
        tau = jnp.where(has_below1, 2.0 / (jnp.sum(v * v, axis=1, keepdims=True) + dead), 0.0)
        ((_, product),) = combined([v], [tau])
        first_product[...] = product[WIDTH:FRAME]


    @pl.when(jnp.logical_not(lower_last))
    def _():
        lower_chain()
        pl.when(has_below1)(halo_copy.wait_recv)
        xe[WIDTH : WIDTH + RIM, :] = xe[WIDTH : WIDTH + RIM, :] - dot(
            first_product[:, 0:FRAME], xe[0:FRAME, :]
        )

    answer = xe[WIDTH : WIDTH + rows, cols:wide]
    head = answer.astype(jnp.bfloat16).astype(F32)
    reply[...] = (
        head + pltpu.roll(head, SLOT, 1) + pltpu.roll(answer - head, 2 * SLOT, 1)
    ).astype(jnp.bfloat16)

    @pl.when(last_below1)
    def _():
        heard(2)
        heads_copy.start()
        near_copy.start()

    @pl.when(last_below2)
    def _():
        heard(3)
        far_copy.start()

    pl.when(has_above1)(near_copy.wait_recv)
    pl.when(has_above2)(far_copy.wait_recv)
    early = RIM - EARLY
    inflow = jnp.concatenate(
        [
            orec[0:early, 0:cols],
            orec[early:RIM, 0:cols] + dot(orec[early:RIM, cols : cols + EARLY], o2rec[...]),
        ],
        axis=0,
    )
    head = inflow.astype(jnp.bfloat16).astype(F32)
    gap = jnp.zeros((SLOT - RIM, cols), F32)
    stack = jnp.concatenate([head, gap, inflow - head, gap, head, gap, jnp.zeros((SLOT, cols), F32)], axis=0)
    y_ref[...] = xe[WIDTH : WIDTH + rows, 0:cols] + jnp.dot(
        reply[...], stack.astype(jnp.bfloat16), preferred_element_type=F32
    )

    @pl.when(lower_last)
    def _():
        lower_chain()
        pl.when(has_below1)(halo_copy.wait_recv)
        frame = jnp.concatenate([xe[0:WIDTH, 0:cols], y_ref[0:RIM, :]], axis=0)
        y_ref[0:RIM, :] = y_ref[0:RIM, :] - dot(first_product[:, 0:FRAME], frame)

    for copy in gathers:
        copy.wait_send()

    pl.when(has_above1)(halo_copy.wait_send)
    pl.when(has_above1 & jnp.logical_not(wide_above1))(tails_copy.wait_send)

    @pl.when(wide_above1)
    def _():
        for copy in tail_copies:
            copy.wait_send()

    @pl.when(has_below1)
    def _():
        heads_copy.wait_send()
        near_copy.wait_send()

    pl.when(has_below2)(far_copy.wait_send)


def local(row_count, col_count, eig_slab, reflectors, row_offsets):
    rows, cols = eig_slab.shape
    per = reflectors.shape[0]
    wide = cols + LANES
    return pl.pallas_call(
        functools.partial(sweep_kernel, row_count, col_count),
        out_shape=jax.ShapeDtypeStruct((rows, cols), F32),
        in_specs=[pl.BlockSpec(memory_space=pltpu.HBM)] * 3,
        out_specs=pl.BlockSpec(memory_space=pltpu.VMEM),
        scratch_shapes=[
            pltpu.SMEM((SWEEPS,), jnp.int32),
            pltpu.VMEM((WIDTH + rows, wide), F32),
            pltpu.VMEM((col_count, per, rows), F32),
            pltpu.VMEM((SWEEPS, rows), F32),
            pltpu.VMEM((SWEEPS, LANES), F32),
            pltpu.VMEM((col_count, per, LANES), F32),
            pltpu.VMEM((SWEEPS, LANES), F32),
            pltpu.VMEM((RIM, wide), F32),
            pltpu.VMEM((EARLY, cols), F32),
            pltpu.VMEM((RIM, wide), F32),
            pltpu.VMEM((EARLY, cols), F32),
            pltpu.VMEM((RIM, LANES), F32),
            pltpu.VMEM((WIDTH, wide), F32),
            pltpu.VMEM((FRAME, LANES), F32),
            pltpu.VMEM(((rows // WIDTH - 2) // 2, WIDTH + FRAME, WIDTH + FRAME), F32),
            pltpu.VMEM((rows, LANES), jnp.bfloat16),
            pltpu.SemaphoreType.DMA((3,)),
            pltpu.SemaphoreType.DMA((col_count,)),
            pltpu.SemaphoreType.DMA((col_count,)),
            pltpu.SemaphoreType.DMA((col_count,)),
            pltpu.SemaphoreType.DMA((col_count,)),
            pltpu.SemaphoreType.DMA((5,)),
            pltpu.SemaphoreType.DMA((5,)),
            pltpu.SemaphoreType.REGULAR((4,)),
        ],
        compiler_params=pltpu.CompilerParams(
            collective_id=0, has_side_effects=True, vmem_limit_bytes=24 * 2**20
        ),
        name="sweep",
    )(*(pltpu.with_memory_space_constraint(a, pltpu.HBM) for a in (row_offsets, reflectors, eig_slab)))


def solution(mesh):
    placed = (P("row", "col"), P("col", "row"), P())
    return jax.shard_map(
        functools.partial(local, mesh.shape["row"], mesh.shape["col"]),
        mesh=mesh, in_specs=placed, out_specs=P("row", "col"), check_vma=False,
    )
```

```python
import functools

import jax
import jax.numpy as jnp
from jax import lax
from jax.experimental import pallas as pl
from jax.experimental.pallas import tpu as pltpu
from jax.sharding import PartitionSpec as P

WIDTH = 64
SWEEPS = 16
RIM = 24
FRAME = WIDTH + RIM
EARLY = 16
LANES = 128
SLOT = 32
TURN = 16
MESH = pl.DeviceIdType.MESH
F32 = jnp.float32
HIGH = lax.Precision.HIGH
HIGHEST = lax.Precision.HIGHEST


def dot(a, b, precision=HIGH):
    return jnp.dot(a, b, precision=precision, preferred_element_type=F32)


def halves(x):
    head = x.astype(jnp.bfloat16)
    return head, (x - head.astype(F32)).astype(jnp.bfloat16)


def substituted(scaled, base, w):
    half = SWEEPS // 2
    top, bottom = w[0:half], w[half:SWEEPS]
    for j in range(SWEEPS - 1):
        column = slice(base + j, base + j + 1)
        if j < half:
            row = top[j : j + 1]
            if j < half - 1:
                top = top - scaled[0:half, column] * row
        else:
            row = bottom[j - half : j - half + 1]
        bottom = bottom - scaled[half:SWEEPS, column] * row
    return jnp.concatenate([top, bottom], axis=0)


def combined(frames, taus):
    v_all = jnp.concatenate(frames, axis=0)
    tau = jnp.concatenate(taus, axis=0)
    n = v_all.shape[0]
    gram = lax.dot_general(
        v_all, v_all, (((1,), (1,)), ((), ())), precision=HIGH, preferred_element_type=F32
    )
    scaled = gram * tau
    w_all = v_all * tau
    out = []
    for i, v in enumerate(frames):
        lo = SWEEPS * i
        block = scaled[lo : lo + SWEEPS, 0:n]
        below = lax.broadcasted_iota(jnp.int32, (SWEEPS, n), 0) > (
            lax.broadcasted_iota(jnp.int32, (SWEEPS, n), 1) - lo
        )
        block = jnp.where(below, block, 0.0)
        w = substituted(block, lo, w_all[lo : lo + SWEEPS])
        vh, vl = halves(v)
        wh, wl = halves(w)
        product = lax.dot_general(
            jnp.concatenate([vh, vh, vl], axis=0), jnp.concatenate([wh, wl, wh], axis=0),
            (((0,), (0,)), ((), ())), preferred_element_type=F32,
        )
        out.append((w, product))
    return out


def paired(upper, lower):
    lanes = upper.shape[1]
    entry = lax.broadcasted_iota(jnp.int32, (RIM, lanes), 0) == lax.broadcasted_iota(
        jnp.int32, (RIM, lanes), 1
    )
    passed = jnp.where(entry, 1.0, 0.0) - upper[0:RIM]
    right = dot(lower[0:FRAME, WIDTH:FRAME], passed)
    right = jnp.concatenate([right[0:WIDTH], right[WIDTH:FRAME] + upper[0:RIM], upper[RIM:FRAME]], axis=0)
    left = jnp.concatenate([lower[0:FRAME, 0:WIDTH], jnp.zeros((WIDTH, WIDTH), F32)], axis=0)
    return jnp.concatenate([left, right[:, 0:FRAME]], axis=1)


def sweep_kernel(
    row_count, col_count,
    off_hbm, refl_hbm, x_hbm,
    y_ref,
    off_ref, xe, vrec, vv, heads, tails, tv, osend, fsend, orec, o2rec, first_product, upper, single, pairs, reply,
    local_sems, send_sems, recv_sems, tail_send, tail_recv, edge_send, edge_recv, ready, answered,
):
    per, rows = refl_hbm.shape
    cols = x_hbm.shape[1]
    wide = cols + LANES
    chains = rows // WIDTH
    b = lax.axis_index("row")
    c = lax.axis_index("col")
    below1, below2 = (b - 1, c), (b - 2, c)
    above1, above2 = (b + 1, c), (b + 2, c)
    has_below1, has_below2 = b >= 1, b >= 2
    has_above1, has_above2 = b < row_count - 1, b < row_count - 2
    place = lax.rem(b, TURN)
    late_below1 = has_below1 & ((place == 0) | (b == 1))
    late_below2 = has_below2 & ((place < 2) | (b == 2))
    late_above1 = has_above1 & (place < TURN - 1) & (b > 0)
    late_above2 = has_above2 & (place < TURN - 2) & (b > 0)
    soon_below1, soon_below2 = has_below1 & jnp.logical_not(late_below1), has_below2 & jnp.logical_not(late_below2)
    soon_above1, soon_above2 = has_above1 & jnp.logical_not(late_above1), has_above2 & jnp.logical_not(late_above2)
    last_below1, last_below2 = late_below1 & (place == 0), late_below2 & (place < 2)
    next_below1, next_below2 = late_below1 & (place > 0), late_below2 & (place > 1)
    lower_last = place == 0
    wide_above1 = soon_above1 & (place == TURN - 1)
    neighbours = (
        (above1, late_above1, soon_above1, 0),
        (above2, late_above2, soon_above2, 1),
        (below1, late_below1, soon_below1, 2),
        (below2, late_below2, soon_below2, 3),
    )

    barrier = pltpu.get_barrier_semaphore()

    def greet(peer):
        pl.semaphore_signal(barrier, inc=1, device_id=peer, device_id_type=MESH)

    def col_at(d):
        return lax.rem(c + d, col_count)

    order = sorted(range(1, col_count), key=lambda d: -min(d, col_count - d))

    def turn_of(col):
        return jnp.where(2 * col <= col_count, 2 * col, 2 * (col_count - col) + 3)

    by_turn = sorted(range(col_count), key=lambda p: 2 * p if 2 * p <= col_count else 2 * (col_count - p) + 3)
    turn = turn_of(c)

    def distance(p):
        return lax.rem(p - c + col_count, col_count)

    @pl.when(wide_above1)
    def _():
        for p in by_turn:
            pl.when(turn_of(p) > turn)(functools.partial(greet, (b, p)))

    @pl.when(jnp.logical_not(wide_above1))
    def _():
        for d in order:
            greet((b, col_at(d)))

    for i, (peer, late, _, _) in enumerate(neighbours):
        if i == 2:
            late = next_below1
        pl.when(late)(functools.partial(greet, peer))

    @pl.when(last_below1)
    def _():
        for d in range(col_count):
            greet((b - 1, col_at(d)))

    refl_copy = pltpu.make_async_copy(refl_hbm, vrec.at[c], local_sems.at[0])
    off_copy = pltpu.make_async_copy(off_hbm, off_ref, local_sems.at[1])
    x_copy = pltpu.make_async_copy(x_hbm, xe.at[WIDTH : WIDTH + rows, 0:cols], local_sems.at[2])
    refl_copy.start()
    off_copy.start()
    x_copy.start()

    xe[:, cols:wide] = jnp.zeros((WIDTH + rows, LANES), F32)
    unit = lax.broadcasted_iota(jnp.int32, (RIM, LANES), 0) == lax.broadcasted_iota(
        jnp.int32, (RIM, LANES), 1
    )
    rim = jnp.concatenate([jnp.zeros((RIM, cols), F32), jnp.where(unit, 1.0, 0.0)], axis=1)

    @pl.when(b == 0)
    def _():
        xe[0:WIDTH, 0:cols] = jnp.zeros((WIDTH, cols), F32)

    @pl.when(b == row_count - 1)
    def _():
        orec[...] = jnp.zeros((RIM, wide), F32)

    @pl.when(b >= row_count - 2)
    def _():
        o2rec[...] = jnp.zeros((EARLY, cols), F32)

    sooner = 0
    for p in by_turn:
        sooner = sooner + (turn_of(p) < turn).astype(jnp.int32)
    greeted = jnp.where(wide_above1, sooner + col_count - 1, col_count - 1)
    for _, _, soon, _ in neighbours:
        greeted = greeted + soon.astype(jnp.int32)
    pl.semaphore_wait(barrier, greeted)

    refl_copy.wait()
    gathers = [
        pltpu.make_async_remote_copy(
            src_ref=vrec.at[c], dst_ref=vrec.at[c], send_sem=send_sems.at[d], recv_sem=recv_sems.at[d],
            device_id=(b, col_at(d)), device_id_type=MESH,
        )
        for d in order
    ]

    def gather_to(p):
        return pltpu.make_async_remote_copy(
            src_ref=vrec.at[c], dst_ref=vrec.at[c],
            send_sem=send_sems.at[distance(p)], recv_sem=recv_sems.at[distance(p)],
            device_id=(b, p), device_id_type=MESH,
        )

    def answer(p):
        gather_to(p).start()
        pl.semaphore_signal(
            answered.at[col_count - distance(p)], inc=1, device_id=(b, p), device_id_type=MESH
        )

    def follow(p):
        pl.semaphore_wait(answered.at[distance(p)], 1)
        gather_to(p).start()

    @pl.when(wide_above1)
    def _():
        for p in by_turn:
            pl.when(turn_of(p) < turn)(functools.partial(answer, p))

    @pl.when(jnp.logical_not(wide_above1))
    def _():
        for copy in gathers:
            copy.start()

    def edge(i, src, dst, peer):
        return pltpu.make_async_remote_copy(
            src_ref=src, dst_ref=dst, send_sem=edge_send.at[i], recv_sem=edge_recv.at[i],
            device_id=peer, device_id_type=MESH,
        )

    halo_copy = edge(0, x_hbm.at[rows - WIDTH : rows, :], xe.at[0:WIDTH, 0:cols], above1)
    tails_copy = edge(1, vrec.at[:, :, rows - LANES : rows], tails, above1)
    tail_copies = [
        pltpu.make_async_remote_copy(
            src_ref=vrec.at[c, :, rows - LANES : rows], dst_ref=tails.at[c],
            send_sem=tail_send.at[d], recv_sem=tail_recv.at[d],
            device_id=(b + 1, col_at(d)), device_id_type=MESH,
        )
        for d in range(col_count)
    ]
    heads_copy = edge(2, vv.at[:, 0:LANES], heads, below1)
    near_copy = edge(3, osend.at[:, 0:cols], orec.at[:, 0:cols], below1)
    early = RIM - EARLY
    reply_copy = edge(5, osend.at[early:RIM, cols:wide], orec.at[early:RIM, cols:wide], below1)
    far_copy = edge(4, fsend, o2rec, below2)

    def tell(i, peer):
        pl.semaphore_signal(ready.at[i], inc=1, device_id=peer, device_id_type=MESH)

    for peer, _, soon, i in neighbours:
        if i != 3:
            pl.when(soon)(functools.partial(tell, (i + 2) % 4, peer))

    def heard(i):
        pl.semaphore_wait(ready.at[i], 1)

    @pl.when(wide_above1)
    def _():
        for copy in tail_copies:
            copy.start()

    pl.when(soon_above1)(halo_copy.start)

    @pl.when(wide_above1)
    def _():
        for p in by_turn:
            pl.when(turn_of(p) > turn)(functools.partial(follow, p))


    off_copy.wait()
    for copy in gathers:
        copy.wait_recv()
    for i in range(col_count):
        vv[i * per : (i + 1) * per, :] = vrec[i]

    pl.when(soon_below1)(heads_copy.start)

    pl.when(soon_above1 & jnp.logical_not(wide_above1))(tails_copy.start)

    def send_up():
        heard(0)
        tails_copy.start()
        halo_copy.start()

    slow_above1 = late_above1 & (place == TURN // 2 - 1)
    pl.when(late_above1 & jnp.logical_not(slow_above1))(send_up)

    sweep_of = lax.broadcasted_iota(jnp.int32, (SWEEPS, LANES), 0)
    lane_of = lax.broadcasted_iota(jnp.int32, (SWEEPS, LANES), 1)
    first = jnp.zeros((SWEEPS, LANES), jnp.int32)
    for s in range(SWEEPS):
        first = jnp.where(sweep_of == s, off_ref[s], first)
    window = (lane_of >= first) & (lane_of < first + WIDTH)

    def inner_frames():
        own = vv[...]
        turned = pltpu.roll(own, rows - WIDTH, 1)
        frames = []
        for k in range(chains - 1):
            lo = WIDTH * k
            v = own[:, lo : lo + LANES] if k % 2 == 0 else turned[:, lo - WIDTH : lo - WIDTH + LANES]
            frames.append(jnp.where(window, v, 0.0))
        return frames, [2.0 / jnp.sum(v * v, axis=1, keepdims=True) for v in frames]

    def upper_frame():
        v = jnp.concatenate([vv[:, rows - WIDTH : rows], heads[:, 0:WIDTH]], axis=1)
        v = jnp.where(window & ((lane_of < WIDTH) | has_above1), v, 0.0)
        return v, 2.0 / jnp.sum(v * v, axis=1, keepdims=True)

    def keep(products):
        single[...] = products[chains - 2][0:FRAME]
        for i, k in enumerate(range(chains - 3, 0, -2)):
            pairs[i] = paired(products[k], products[k - 1])

    def run_upper(product):
        raw = xe[top : top + WIDTH, :]
        upper[...] = raw - dot(product[0:WIDTH, 0:FRAME], jnp.concatenate([raw, rim], axis=0))

    top = rows
    x_copy.wait()

    prompt = lax.rem(b, 2) == 0

    @pl.when(prompt)
    def _():
        pl.when(has_above1)(heads_copy.wait_recv)
        frames, taus = inner_frames()
        v, tau = upper_frame()
        products = [product for _, product in combined(frames + [v], taus + [tau])]
        run_upper(products[chains - 1])
        keep(products)

    @pl.when(jnp.logical_not(prompt))
    def _():
        keep([product for _, product in combined(*inner_frames())])

    @pl.when(next_below1)
    def _():
        heard(2)
        heads_copy.start()

    frame = jnp.concatenate([xe[top - WIDTH : top, :], rim], axis=0)
    frame = frame - dot(single[:, 0:FRAME], frame)
    xe[top - WIDTH : top, :] = frame[0:WIDTH]
    above = frame[WIDTH:FRAME]
    span = WIDTH + FRAME
    for i, k in enumerate(range(chains - 3, 0, -2)):
        lo = WIDTH * k
        frame = xe[lo : lo + span, :]
        xe[lo : lo + span, :] = frame - dot(pairs[i], frame)

    def send_far():
        pl.when(next_below2)(lambda: heard(3))
        pl.when(soon_below2 | next_below2)(far_copy.start)

    def set_far():
        fsend[...] = xe[WIDTH : WIDTH + EARLY, 0:cols] + dot(
            xe[WIDTH : WIDTH + EARLY, cols : cols + RIM], xe[top : top + RIM, 0:cols]
        )

    def set_near():
        flow = jnp.concatenate(
            [xe[WIDTH : WIDTH + RIM, 0:cols], jnp.zeros((RIM, LANES), F32)], axis=1
        ) + dot(xe[WIDTH : WIDTH + RIM, cols : cols + RIM], upper[0:RIM, :])
        osend[...] = flow

    near_now = soon_below1 | next_below1

    @pl.when(prompt)
    def _():
        set_far()
        set_near()
        pl.when(near_now)(reply_copy.start)
        send_far()
        pl.when(near_now)(near_copy.start)

    @pl.when(jnp.logical_not(prompt))
    def _():
        set_far()
        send_far()
        pl.when(slow_above1)(send_up)
        pl.when(has_above1)(heads_copy.wait_recv)
        v, tau = upper_frame()
        ((_, product),) = combined([v], [tau])
        run_upper(product)
        set_near()

        @pl.when(near_now)
        def _():
            reply_copy.start()
            near_copy.start()

    carried = jnp.concatenate([xe[WIDTH + RIM : top, :], above], axis=0)
    xe[WIDTH : WIDTH + RIM, :] = osend[...]
    moved = dot(carried[:, cols : cols + RIM], upper[0:RIM, :])
    xe[WIDTH + RIM : top + RIM, 0:cols] = carried[:, 0:cols] + moved[:, 0:cols]
    xe[WIDTH + RIM : top + RIM, cols:wide] = moved[:, cols:wide]
    xe[top + RIM : top + WIDTH, :] = upper[RIM:WIDTH, :]

    def lower_chain():
        pl.when(has_below1 & jnp.logical_not(last_below1))(tails_copy.wait_recv)

        @pl.when(last_below1)
        def _():
            for copy in tail_copies:
                copy.wait_recv()

        for i in range(col_count):
            tv[i * per : (i + 1) * per, :] = tails[i]
        v = jnp.concatenate([tv[:, WIDTH:LANES], vv[:, 0:WIDTH]], axis=1)
        v = jnp.where(window & has_below1, v, 0.0)
        dead = jnp.where(has_below1, 0.0, 1.0)
        tau = jnp.where(has_below1, 2.0 / (jnp.sum(v * v, axis=1, keepdims=True) + dead), 0.0)
        ((_, product),) = combined([v], [tau])
        first_product[...] = product[WIDTH:FRAME]


    @pl.when(jnp.logical_not(lower_last))
    def _():
        lower_chain()
        pl.when(has_below1)(halo_copy.wait_recv)
        xe[WIDTH : WIDTH + RIM, :] = xe[WIDTH : WIDTH + RIM, :] - dot(
            first_product[:, 0:FRAME], xe[0:FRAME, :]
        )

    answer = xe[WIDTH : WIDTH + rows, cols:wide]
    head = answer.astype(jnp.bfloat16).astype(F32)
    reply[...] = (
        head + pltpu.roll(head, SLOT, 1) + pltpu.roll(answer - head, 2 * SLOT, 1)
    ).astype(jnp.bfloat16)

    @pl.when(last_below1)
    def _():
        heard(2)
        heads_copy.start()
        reply_copy.start()
        near_copy.start()

    @pl.when(last_below2)
    def _():
        heard(3)
        far_copy.start()

    pl.when(has_above1)(reply_copy.wait_recv)
    pl.when(has_above2)(far_copy.wait_recv)
    passed = dot(orec[early:RIM, cols : cols + EARLY], o2rec[...])
    pl.when(has_above1)(near_copy.wait_recv)
    inflow = jnp.concatenate(
        [orec[0:early, 0:cols], orec[early:RIM, 0:cols] + passed], axis=0
    )
    head = inflow.astype(jnp.bfloat16).astype(F32)
    gap = jnp.zeros((SLOT - RIM, cols), F32)
    stack = jnp.concatenate([head, gap, inflow - head, gap, head, gap, jnp.zeros((SLOT, cols), F32)], axis=0)
    y_ref[...] = xe[WIDTH : WIDTH + rows, 0:cols] + jnp.dot(
        reply[...], stack.astype(jnp.bfloat16), preferred_element_type=F32
    )

    @pl.when(lower_last)
    def _():
        lower_chain()
        pl.when(has_below1)(halo_copy.wait_recv)
        frame = jnp.concatenate([xe[0:WIDTH, 0:cols], y_ref[0:RIM, :]], axis=0)
        y_ref[0:RIM, :] = y_ref[0:RIM, :] - dot(first_product[:, 0:FRAME], frame)

    for copy in gathers:
        copy.wait_send()

    pl.when(has_above1)(halo_copy.wait_send)
    pl.when(has_above1 & jnp.logical_not(wide_above1))(tails_copy.wait_send)

    @pl.when(wide_above1)
    def _():
        for copy in tail_copies:
            copy.wait_send()

    @pl.when(has_below1)
    def _():
        heads_copy.wait_send()
        reply_copy.wait_send()
        near_copy.wait_send()

    pl.when(has_below2)(far_copy.wait_send)


def local(row_count, col_count, eig_slab, reflectors, row_offsets):
    rows, cols = eig_slab.shape
    per = reflectors.shape[0]
    wide = cols + LANES
    return pl.pallas_call(
        functools.partial(sweep_kernel, row_count, col_count),
        out_shape=jax.ShapeDtypeStruct((rows, cols), F32),
        in_specs=[pl.BlockSpec(memory_space=pltpu.HBM)] * 3,
        out_specs=pl.BlockSpec(memory_space=pltpu.VMEM),
        scratch_shapes=[
            pltpu.SMEM((SWEEPS,), jnp.int32),
            pltpu.VMEM((WIDTH + rows, wide), F32),
            pltpu.VMEM((col_count, per, rows), F32),
            pltpu.VMEM((SWEEPS, rows), F32),
            pltpu.VMEM((SWEEPS, LANES), F32),
            pltpu.VMEM((col_count, per, LANES), F32),
            pltpu.VMEM((SWEEPS, LANES), F32),
            pltpu.VMEM((RIM, wide), F32),
            pltpu.VMEM((EARLY, cols), F32),
            pltpu.VMEM((RIM, wide), F32),
            pltpu.VMEM((EARLY, cols), F32),
            pltpu.VMEM((RIM, LANES), F32),
            pltpu.VMEM((WIDTH, wide), F32),
            pltpu.VMEM((FRAME, LANES), F32),
            pltpu.VMEM(((rows // WIDTH - 2) // 2, WIDTH + FRAME, WIDTH + FRAME), F32),
            pltpu.VMEM((rows, LANES), jnp.bfloat16),
            pltpu.SemaphoreType.DMA((3,)),
            pltpu.SemaphoreType.DMA((col_count,)),
            pltpu.SemaphoreType.DMA((col_count,)),
            pltpu.SemaphoreType.DMA((col_count,)),
            pltpu.SemaphoreType.DMA((col_count,)),
            pltpu.SemaphoreType.DMA((6,)),
            pltpu.SemaphoreType.DMA((6,)),
            pltpu.SemaphoreType.REGULAR((4,)),
            pltpu.SemaphoreType.REGULAR((col_count,)),
        ],
        compiler_params=pltpu.CompilerParams(
            collective_id=0, has_side_effects=True, vmem_limit_bytes=24 * 2**20
        ),
        name="sweep",
    )(*(pltpu.with_memory_space_constraint(a, pltpu.HBM) for a in (row_offsets, reflectors, eig_slab)))


def solution(mesh):
    placed = (P("row", "col"), P("col", "row"), P())
    return jax.shard_map(
        functools.partial(local, mesh.shape["row"], mesh.shape["col"]),
        mesh=mesh, in_specs=placed, out_specs=P("row", "col"), check_vma=False,
    )
```

```python
import functools

import jax
import jax.numpy as jnp
from jax import lax
from jax.experimental import pallas as pl
from jax.experimental.pallas import tpu as pltpu
from jax.sharding import PartitionSpec as P

WIDTH = 64
SWEEPS = 16
RIM = 24
FRAME = WIDTH + RIM
EARLY = 16
LANES = 128
SLOT = 32
TURN = 16
MESH = pl.DeviceIdType.MESH
F32 = jnp.float32
HIGH = lax.Precision.HIGH
HIGHEST = lax.Precision.HIGHEST


def dot(a, b, precision=HIGH):
    return jnp.dot(a, b, precision=precision, preferred_element_type=F32)


def halves(x):
    head = x.astype(jnp.bfloat16)
    return head, (x - head.astype(F32)).astype(jnp.bfloat16)


def substituted(scaled, base, w):
    half = SWEEPS // 2
    top, bottom = w[0:half], w[half:SWEEPS]
    for j in range(SWEEPS - 1):
        column = slice(base + j, base + j + 1)
        if j < half:
            row = top[j : j + 1]
            if j < half - 1:
                top = top - scaled[0:half, column] * row
        else:
            row = bottom[j - half : j - half + 1]
        bottom = bottom - scaled[half:SWEEPS, column] * row
    return jnp.concatenate([top, bottom], axis=0)


def combined(frames, taus):
    v_all = jnp.concatenate(frames, axis=0)
    tau = jnp.concatenate(taus, axis=0)
    n = v_all.shape[0]
    gram = lax.dot_general(
        v_all, v_all, (((1,), (1,)), ((), ())), precision=HIGH, preferred_element_type=F32
    )
    scaled = gram * tau
    w_all = v_all * tau
    out = []
    for i, v in enumerate(frames):
        lo = SWEEPS * i
        block = scaled[lo : lo + SWEEPS, 0:n]
        below = lax.broadcasted_iota(jnp.int32, (SWEEPS, n), 0) > (
            lax.broadcasted_iota(jnp.int32, (SWEEPS, n), 1) - lo
        )
        block = jnp.where(below, block, 0.0)
        w = substituted(block, lo, w_all[lo : lo + SWEEPS])
        vh, vl = halves(v)
        wh, wl = halves(w)
        product = lax.dot_general(
            jnp.concatenate([vh, vh, vl], axis=0), jnp.concatenate([wh, wl, wh], axis=0),
            (((0,), (0,)), ((), ())), preferred_element_type=F32,
        )
        out.append((w, product))
    return out


def paired(upper, lower):
    lanes = upper.shape[1]
    entry = lax.broadcasted_iota(jnp.int32, (RIM, lanes), 0) == lax.broadcasted_iota(
        jnp.int32, (RIM, lanes), 1
    )
    passed = jnp.where(entry, 1.0, 0.0) - upper[0:RIM]
    right = dot(lower[0:FRAME, WIDTH:FRAME], passed)
    right = jnp.concatenate([right[0:WIDTH], right[WIDTH:FRAME] + upper[0:RIM], upper[RIM:FRAME]], axis=0)
    left = jnp.concatenate([lower[0:FRAME, 0:WIDTH], jnp.zeros((WIDTH, WIDTH), F32)], axis=0)
    return jnp.concatenate([left, right[:, 0:FRAME]], axis=1)


def sweep_kernel(
    row_count, col_count,
    off_hbm, refl_hbm, x_hbm,
    y_ref,
    off_ref, xe, vrec, vv, heads, tails, tv, osend, fsend, orec, o2rec, first_product, upper, single, pairs, reply,
    local_sems, send_sems, recv_sems, tail_send, tail_recv, edge_send, edge_recv, ready, answered,
):
    per, rows = refl_hbm.shape
    cols = x_hbm.shape[1]
    wide = cols + LANES
    chains = rows // WIDTH
    b = lax.axis_index("row")
    c = lax.axis_index("col")
    below1, below2 = (b - 1, c), (b - 2, c)
    above1, above2 = (b + 1, c), (b + 2, c)
    has_below1, has_below2 = b >= 1, b >= 2
    has_above1, has_above2 = b < row_count - 1, b < row_count - 2
    place = lax.rem(b, TURN)
    late_below1 = has_below1 & ((place == 0) | (b == 1))
    late_below2 = has_below2 & ((place < 2) | (b == 2))
    late_above1 = has_above1 & (place < TURN - 1) & (b > 0)
    late_above2 = has_above2 & (place < TURN - 2) & (b > 0)
    soon_below1, soon_below2 = has_below1 & jnp.logical_not(late_below1), has_below2 & jnp.logical_not(late_below2)
    soon_above1, soon_above2 = has_above1 & jnp.logical_not(late_above1), has_above2 & jnp.logical_not(late_above2)
    last_below1, last_below2 = late_below1 & (place == 0), late_below2 & (place < 2)
    next_below1, next_below2 = late_below1 & (place > 0), late_below2 & (place > 1)
    lower_last = place == 0
    wide_above1 = soon_above1 & (place == TURN - 1)
    neighbours = (
        (above1, late_above1, soon_above1, 0),
        (above2, late_above2, soon_above2, 1),
        (below1, late_below1, soon_below1, 2),
        (below2, late_below2, soon_below2, 3),
    )

    barrier = pltpu.get_barrier_semaphore()

    def greet(peer):
        pl.semaphore_signal(barrier, inc=1, device_id=peer, device_id_type=MESH)

    def col_at(d):
        return lax.rem(c + d, col_count)

    order = sorted(range(1, col_count), key=lambda d: -min(d, col_count - d))

    def turn_of(col):
        return jnp.where(2 * col <= col_count, 2 * col, 2 * (col_count - col) + 3)

    by_turn = sorted(range(col_count), key=lambda p: 2 * p if 2 * p <= col_count else 2 * (col_count - p) + 3)
    turn = turn_of(c)

    def distance(p):
        return lax.rem(p - c + col_count, col_count)

    @pl.when(wide_above1)
    def _():
        for p in by_turn:
            pl.when(turn_of(p) > turn)(functools.partial(greet, (b, p)))

    @pl.when(jnp.logical_not(wide_above1))
    def _():
        for d in order:
            greet((b, col_at(d)))

    for i, (peer, late, _, _) in enumerate(neighbours):
        if i == 2:
            late = next_below1
        pl.when(late)(functools.partial(greet, peer))

    @pl.when(last_below1)
    def _():
        for d in range(col_count):
            greet((b - 1, col_at(d)))

    refl_copy = pltpu.make_async_copy(refl_hbm, vrec.at[c], local_sems.at[0])
    off_copy = pltpu.make_async_copy(off_hbm, off_ref, local_sems.at[1])
    x_copy = pltpu.make_async_copy(x_hbm, xe.at[WIDTH : WIDTH + rows, 0:cols], local_sems.at[2])
    refl_copy.start()
    off_copy.start()
    x_copy.start()

    xe[:, cols:wide] = jnp.zeros((WIDTH + rows, LANES), F32)
    unit = lax.broadcasted_iota(jnp.int32, (RIM, LANES), 0) == lax.broadcasted_iota(
        jnp.int32, (RIM, LANES), 1
    )
    rim = jnp.concatenate([jnp.zeros((RIM, cols), F32), jnp.where(unit, 1.0, 0.0)], axis=1)

    @pl.when(b == 0)
    def _():
        xe[0:WIDTH, 0:cols] = jnp.zeros((WIDTH, cols), F32)

    @pl.when(b == row_count - 1)
    def _():
        orec[...] = jnp.zeros((RIM, wide), F32)

    @pl.when(b >= row_count - 2)
    def _():
        o2rec[...] = jnp.zeros((EARLY, cols), F32)

    sooner = 0
    for p in by_turn:
        sooner = sooner + (turn_of(p) < turn).astype(jnp.int32)
    greeted = jnp.where(wide_above1, sooner + col_count - 1, col_count - 1)
    for _, _, soon, _ in neighbours:
        greeted = greeted + soon.astype(jnp.int32)
    pl.semaphore_wait(barrier, greeted)

    refl_copy.wait()
    gathers = [
        pltpu.make_async_remote_copy(
            src_ref=vrec.at[c], dst_ref=vrec.at[c], send_sem=send_sems.at[d], recv_sem=recv_sems.at[d],
            device_id=(b, col_at(d)), device_id_type=MESH,
        )
        for d in order
    ]

    def gather_to(p):
        return pltpu.make_async_remote_copy(
            src_ref=vrec.at[c], dst_ref=vrec.at[c],
            send_sem=send_sems.at[distance(p)], recv_sem=recv_sems.at[distance(p)],
            device_id=(b, p), device_id_type=MESH,
        )

    def answer(p):
        gather_to(p).start()
        pl.semaphore_signal(
            answered.at[col_count - distance(p)], inc=1, device_id=(b, p), device_id_type=MESH
        )

    def follow(p):
        pl.semaphore_wait(answered.at[distance(p)], 1)
        gather_to(p).start()

    @pl.when(wide_above1)
    def _():
        for p in by_turn:
            pl.when(turn_of(p) < turn)(functools.partial(answer, p))

    @pl.when(jnp.logical_not(wide_above1))
    def _():
        for copy in gathers:
            copy.start()

    def edge(i, src, dst, peer):
        return pltpu.make_async_remote_copy(
            src_ref=src, dst_ref=dst, send_sem=edge_send.at[i], recv_sem=edge_recv.at[i],
            device_id=peer, device_id_type=MESH,
        )

    halo_copy = edge(0, x_hbm.at[rows - WIDTH : rows, :], xe.at[0:WIDTH, 0:cols], above1)
    tails_copy = edge(1, vrec.at[:, :, rows - LANES : rows], tails, above1)
    tail_copies = [
        pltpu.make_async_remote_copy(
            src_ref=vrec.at[c, :, rows - LANES : rows], dst_ref=tails.at[c],
            send_sem=tail_send.at[d], recv_sem=tail_recv.at[d],
            device_id=(b + 1, col_at(d)), device_id_type=MESH,
        )
        for d in range(col_count)
    ]
    heads_copy = edge(2, vv.at[:, 0:LANES], heads, below1)
    near_copy = edge(3, osend.at[:, 0:cols], orec.at[:, 0:cols], below1)
    early = RIM - EARLY
    reply_copy = edge(5, osend.at[early:RIM, cols:wide], orec.at[early:RIM, cols:wide], below1)
    far_copy = edge(4, fsend, o2rec, below2)

    def tell(i, peer):
        pl.semaphore_signal(ready.at[i], inc=1, device_id=peer, device_id_type=MESH)

    for peer, _, soon, i in neighbours:
        if i != 3:
            pl.when(soon)(functools.partial(tell, (i + 2) % 4, peer))

    def heard(i):
        pl.semaphore_wait(ready.at[i], 1)

    @pl.when(wide_above1)
    def _():
        for copy in tail_copies:
            copy.start()

    pl.when(soon_above1)(halo_copy.start)

    @pl.when(wide_above1)
    def _():
        for p in by_turn:
            pl.when(turn_of(p) > turn)(functools.partial(follow, p))


    off_copy.wait()
    for copy in gathers:
        copy.wait_recv()
    for i in range(col_count):
        vv[i * per : (i + 1) * per, :] = vrec[i]

    pl.when(soon_below1)(heads_copy.start)

    pl.when(soon_above1 & jnp.logical_not(wide_above1))(tails_copy.start)

    def send_up():
        heard(0)
        tails_copy.start()
        halo_copy.start()

    slow_above1 = late_above1 & (place == TURN // 2 - 1)
    pl.when(late_above1 & jnp.logical_not(slow_above1))(send_up)

    sweep_of = lax.broadcasted_iota(jnp.int32, (SWEEPS, LANES), 0)
    lane_of = lax.broadcasted_iota(jnp.int32, (SWEEPS, LANES), 1)
    first = jnp.zeros((SWEEPS, LANES), jnp.int32)
    for s in range(SWEEPS):
        first = jnp.where(sweep_of == s, off_ref[s], first)
    window = (lane_of >= first) & (lane_of < first + WIDTH)

    def inner_frames():
        own = vv[...]
        turned = pltpu.roll(own, rows - WIDTH, 1)
        frames = []
        for k in range(chains - 1):
            lo = WIDTH * k
            v = own[:, lo : lo + LANES] if k % 2 == 0 else turned[:, lo - WIDTH : lo - WIDTH + LANES]
            frames.append(jnp.where(window, v, 0.0))
        return frames, [2.0 / jnp.sum(v * v, axis=1, keepdims=True) for v in frames]

    def upper_frame():
        v = jnp.concatenate([vv[:, rows - WIDTH : rows], heads[:, 0:WIDTH]], axis=1)
        v = jnp.where(window & ((lane_of < WIDTH) | has_above1), v, 0.0)
        return v, 2.0 / jnp.sum(v * v, axis=1, keepdims=True)

    def keep(products):
        single[...] = products[chains - 2][0:FRAME]
        for i, k in enumerate(range(chains - 3, 0, -2)):
            pairs[i] = paired(products[k], products[k - 1])

    def run_upper(product):
        raw = xe[top : top + WIDTH, :]
        upper[...] = raw - dot(product[0:WIDTH, 0:FRAME], jnp.concatenate([raw, rim], axis=0))

    top = rows
    x_copy.wait()

    prompt = lax.rem(b, 2) == 0

    @pl.when(prompt)
    def _():
        pl.when(has_above1)(heads_copy.wait_recv)
        frames, taus = inner_frames()
        v, tau = upper_frame()
        frames, taus = frames + [v], taus + [tau]
        half = chains // 2
        products = [p for _, p in combined(frames[:half], taus[:half]) + combined(frames[half:], taus[half:])]
        run_upper(products[chains - 1])
        keep(products)

    @pl.when(jnp.logical_not(prompt))
    def _():
        keep([product for _, product in combined(*inner_frames())])

    @pl.when(next_below1)
    def _():
        heard(2)
        heads_copy.start()

    frame = jnp.concatenate([xe[top - WIDTH : top, :], rim], axis=0)
    frame = frame - dot(single[:, 0:FRAME], frame)
    xe[top - WIDTH : top, :] = frame[0:WIDTH]
    above = frame[WIDTH:FRAME]
    span = WIDTH + FRAME
    for i, k in enumerate(range(chains - 3, 0, -2)):
        lo = WIDTH * k
        frame = xe[lo : lo + span, :]
        xe[lo : lo + span, :] = frame - dot(pairs[i], frame)

    def send_far():
        pl.when(next_below2)(lambda: heard(3))
        pl.when(soon_below2 | next_below2)(far_copy.start)

    def set_far():
        fsend[...] = xe[WIDTH : WIDTH + EARLY, 0:cols] + dot(
            xe[WIDTH : WIDTH + EARLY, cols : cols + RIM], xe[top : top + RIM, 0:cols]
        )

    def set_near():
        flow = jnp.concatenate(
            [xe[WIDTH : WIDTH + RIM, 0:cols], jnp.zeros((RIM, LANES), F32)], axis=1
        ) + dot(xe[WIDTH : WIDTH + RIM, cols : cols + RIM], upper[0:RIM, :])
        osend[...] = flow

    near_now = soon_below1 | next_below1

    @pl.when(prompt)
    def _():
        set_far()
        set_near()
        pl.when(near_now)(reply_copy.start)
        send_far()
        pl.when(near_now)(near_copy.start)

    @pl.when(jnp.logical_not(prompt))
    def _():
        set_far()
        send_far()
        pl.when(slow_above1)(send_up)
        pl.when(has_above1)(heads_copy.wait_recv)
        v, tau = upper_frame()
        ((_, product),) = combined([v], [tau])
        run_upper(product)
        set_near()

        @pl.when(near_now)
        def _():
            reply_copy.start()
            near_copy.start()

    carried = jnp.concatenate([xe[WIDTH + RIM : top, :], above], axis=0)
    xe[WIDTH : WIDTH + RIM, :] = osend[...]
    moved = dot(carried[:, cols : cols + RIM], upper[0:RIM, :])
    xe[WIDTH + RIM : top + RIM, 0:cols] = carried[:, 0:cols] + moved[:, 0:cols]
    xe[WIDTH + RIM : top + RIM, cols:wide] = moved[:, cols:wide]
    xe[top + RIM : top + WIDTH, :] = upper[RIM:WIDTH, :]

    def lower_chain():
        pl.when(has_below1 & jnp.logical_not(last_below1))(tails_copy.wait_recv)

        @pl.when(last_below1)
        def _():
            for copy in tail_copies:
                copy.wait_recv()

        for i in range(col_count):
            tv[i * per : (i + 1) * per, :] = tails[i]
        v = jnp.concatenate([tv[:, WIDTH:LANES], vv[:, 0:WIDTH]], axis=1)
        v = jnp.where(window & has_below1, v, 0.0)
        dead = jnp.where(has_below1, 0.0, 1.0)
        tau = jnp.where(has_below1, 2.0 / (jnp.sum(v * v, axis=1, keepdims=True) + dead), 0.0)
        ((_, product),) = combined([v], [tau])
        first_product[...] = product[WIDTH:FRAME]


    @pl.when(jnp.logical_not(lower_last))
    def _():
        lower_chain()
        pl.when(has_below1)(halo_copy.wait_recv)
        xe[WIDTH : WIDTH + RIM, :] = xe[WIDTH : WIDTH + RIM, :] - dot(
            first_product[:, 0:FRAME], xe[0:FRAME, :]
        )

    answer = xe[WIDTH : WIDTH + rows, cols:wide]
    head = answer.astype(jnp.bfloat16).astype(F32)
    reply[...] = (
        head + pltpu.roll(head, SLOT, 1) + pltpu.roll(answer - head, 2 * SLOT, 1)
    ).astype(jnp.bfloat16)

    @pl.when(last_below1)
    def _():
        heard(2)
        heads_copy.start()
        reply_copy.start()
        near_copy.start()

    @pl.when(last_below2)
    def _():
        heard(3)
        far_copy.start()

    pl.when(has_above1)(reply_copy.wait_recv)
    pl.when(has_above2)(far_copy.wait_recv)
    passed = dot(orec[early:RIM, cols : cols + EARLY], o2rec[...])
    pl.when(has_above1)(near_copy.wait_recv)
    inflow = jnp.concatenate(
        [orec[0:early, 0:cols], orec[early:RIM, 0:cols] + passed], axis=0
    )
    head = inflow.astype(jnp.bfloat16).astype(F32)
    gap = jnp.zeros((SLOT - RIM, cols), F32)
    stack = jnp.concatenate([head, gap, inflow - head, gap, head, gap, jnp.zeros((SLOT, cols), F32)], axis=0)
    y_ref[...] = xe[WIDTH : WIDTH + rows, 0:cols] + jnp.dot(
        reply[...], stack.astype(jnp.bfloat16), preferred_element_type=F32
    )

    @pl.when(lower_last)
    def _():
        lower_chain()
        pl.when(has_below1)(halo_copy.wait_recv)
        frame = jnp.concatenate([xe[0:WIDTH, 0:cols], y_ref[0:RIM, :]], axis=0)
        y_ref[0:RIM, :] = y_ref[0:RIM, :] - dot(first_product[:, 0:FRAME], frame)

    for copy in gathers:
        copy.wait_send()

    pl.when(has_above1)(halo_copy.wait_send)
    pl.when(has_above1 & jnp.logical_not(wide_above1))(tails_copy.wait_send)

    @pl.when(wide_above1)
    def _():
        for copy in tail_copies:
            copy.wait_send()

    @pl.when(has_below1)
    def _():
        heads_copy.wait_send()
        reply_copy.wait_send()
        near_copy.wait_send()

    pl.when(has_below2)(far_copy.wait_send)


def local(row_count, col_count, eig_slab, reflectors, row_offsets):
    rows, cols = eig_slab.shape
    per = reflectors.shape[0]
    wide = cols + LANES
    return pl.pallas_call(
        functools.partial(sweep_kernel, row_count, col_count),
        out_shape=jax.ShapeDtypeStruct((rows, cols), F32),
        in_specs=[pl.BlockSpec(memory_space=pltpu.HBM)] * 3,
        out_specs=pl.BlockSpec(memory_space=pltpu.VMEM),
        scratch_shapes=[
            pltpu.SMEM((SWEEPS,), jnp.int32),
            pltpu.VMEM((WIDTH + rows, wide), F32),
            pltpu.VMEM((col_count, per, rows), F32),
            pltpu.VMEM((SWEEPS, rows), F32),
            pltpu.VMEM((SWEEPS, LANES), F32),
            pltpu.VMEM((col_count, per, LANES), F32),
            pltpu.VMEM((SWEEPS, LANES), F32),
            pltpu.VMEM((RIM, wide), F32),
            pltpu.VMEM((EARLY, cols), F32),
            pltpu.VMEM((RIM, wide), F32),
            pltpu.VMEM((EARLY, cols), F32),
            pltpu.VMEM((RIM, LANES), F32),
            pltpu.VMEM((WIDTH, wide), F32),
            pltpu.VMEM((FRAME, LANES), F32),
            pltpu.VMEM(((rows // WIDTH - 2) // 2, WIDTH + FRAME, WIDTH + FRAME), F32),
            pltpu.VMEM((rows, LANES), jnp.bfloat16),
            pltpu.SemaphoreType.DMA((3,)),
            pltpu.SemaphoreType.DMA((col_count,)),
            pltpu.SemaphoreType.DMA((col_count,)),
            pltpu.SemaphoreType.DMA((col_count,)),
            pltpu.SemaphoreType.DMA((col_count,)),
            pltpu.SemaphoreType.DMA((6,)),
            pltpu.SemaphoreType.DMA((6,)),
            pltpu.SemaphoreType.REGULAR((4,)),
            pltpu.SemaphoreType.REGULAR((col_count,)),
        ],
        compiler_params=pltpu.CompilerParams(
            collective_id=0, has_side_effects=True, vmem_limit_bytes=24 * 2**20
        ),
        name="sweep",
    )(*(pltpu.with_memory_space_constraint(a, pltpu.HBM) for a in (row_offsets, reflectors, eig_slab)))


def solution(mesh):
    placed = (P("row", "col"), P("col", "row"), P())
    return jax.shard_map(
        functools.partial(local, mesh.shape["row"], mesh.shape["col"]),
        mesh=mesh, in_specs=placed, out_specs=P("row", "col"), check_vma=False,
    )
```

```python
import functools

import jax
import jax.numpy as jnp
from jax import lax
from jax.experimental import pallas as pl
from jax.experimental.pallas import tpu as pltpu
from jax.sharding import PartitionSpec as P

WIDTH = 64
SWEEPS = 16
RIM = 24
FRAME = WIDTH + RIM
EARLY = 16
LANES = 128
SLOT = 32
TURN = 16
MESH = pl.DeviceIdType.MESH
F32 = jnp.float32
HIGH = lax.Precision.HIGH
HIGHEST = lax.Precision.HIGHEST


def dot(a, b, precision=HIGH):
    return jnp.dot(a, b, precision=precision, preferred_element_type=F32)


def halves(x):
    head = x.astype(jnp.bfloat16)
    return head, (x - head.astype(F32)).astype(jnp.bfloat16)


def scaled_rows(v, dead=0.0):
    v = v * lax.rsqrt(jnp.sum(v * v, axis=1, keepdims=True) + dead)
    return v, 2.0 / (jnp.sum(v * v, axis=1, keepdims=True) + dead)


def substituted(scaled, base, w):
    half = SWEEPS // 2
    top, bottom = w[0:half], w[half:SWEEPS]
    for j in range(SWEEPS - 1):
        column = slice(base + j, base + j + 1)
        if j < half:
            row = top[j : j + 1]
            if j < half - 1:
                top = top - scaled[0:half, column] * row
        else:
            row = bottom[j - half : j - half + 1]
        bottom = bottom - scaled[half:SWEEPS, column] * row
    return jnp.concatenate([top, bottom], axis=0)


def combined(frames, taus):
    v_all = jnp.concatenate(frames, axis=0)
    tau = jnp.concatenate(taus, axis=0)
    n = v_all.shape[0]
    gram = lax.dot_general(
        v_all, v_all, (((1,), (1,)), ((), ())), precision=HIGH, preferred_element_type=F32
    )
    scaled = gram * tau
    w_all = v_all * tau
    out = []
    for i, v in enumerate(frames):
        lo = SWEEPS * i
        block = scaled[lo : lo + SWEEPS, 0:n]
        below = lax.broadcasted_iota(jnp.int32, (SWEEPS, n), 0) > (
            lax.broadcasted_iota(jnp.int32, (SWEEPS, n), 1) - lo
        )
        block = jnp.where(below, block, 0.0)
        w = substituted(block, lo, w_all[lo : lo + SWEEPS])
        vh, vl = halves(v)
        wh, wl = halves(w)
        product = lax.dot_general(
            jnp.concatenate([vh, vh, vl], axis=0), jnp.concatenate([wh, wl, wh], axis=0),
            (((0,), (0,)), ((), ())), preferred_element_type=F32,
        )
        out.append((w, product))
    return out


def paired(upper, lower):
    lanes = upper.shape[1]
    entry = lax.broadcasted_iota(jnp.int32, (RIM, lanes), 0) == lax.broadcasted_iota(
        jnp.int32, (RIM, lanes), 1
    )
    passed = jnp.where(entry, 1.0, 0.0) - upper[0:RIM]
    right = dot(lower[0:FRAME, WIDTH:FRAME], passed)
    right = jnp.concatenate([right[0:WIDTH], right[WIDTH:FRAME] + upper[0:RIM], upper[RIM:FRAME]], axis=0)
    left = jnp.concatenate([lower[0:FRAME, 0:WIDTH], jnp.zeros((WIDTH, WIDTH), F32)], axis=0)
    return jnp.concatenate([left, right[:, 0:FRAME]], axis=1)


def sweep_kernel(
    row_count, col_count,
    off_hbm, refl_hbm, x_hbm,
    y_ref,
    off_ref, xe, vrec, vv, heads, tails, tv, osend, fsend, orec, o2rec, first_product, upper, single, pairs, reply,
    local_sems, send_sems, recv_sems, tail_send, tail_recv, edge_send, edge_recv, ready, answered,
):
    per, rows = refl_hbm.shape
    cols = x_hbm.shape[1]
    wide = cols + LANES
    chains = rows // WIDTH
    b = lax.axis_index("row")
    c = lax.axis_index("col")
    below1, below2 = (b - 1, c), (b - 2, c)
    above1, above2 = (b + 1, c), (b + 2, c)
    has_below1, has_below2 = b >= 1, b >= 2
    has_above1, has_above2 = b < row_count - 1, b < row_count - 2
    place = lax.rem(b, TURN)
    late_below1 = has_below1 & ((place == 0) | (b == 1))
    late_below2 = has_below2 & ((place < 2) | (b == 2))
    late_above1 = has_above1 & (place < TURN - 1) & (b > 0)
    late_above2 = has_above2 & (place < TURN - 2) & (b > 0)
    soon_below1, soon_below2 = has_below1 & jnp.logical_not(late_below1), has_below2 & jnp.logical_not(late_below2)
    soon_above1, soon_above2 = has_above1 & jnp.logical_not(late_above1), has_above2 & jnp.logical_not(late_above2)
    last_below1, last_below2 = late_below1 & (place == 0), late_below2 & (place < 2)
    next_below1, next_below2 = late_below1 & (place > 0), late_below2 & (place > 1)
    lower_last = place == 0
    wide_above1 = soon_above1 & (place == TURN - 1)
    neighbours = (
        (above1, late_above1, soon_above1, 0),
        (above2, late_above2, soon_above2, 1),
        (below1, late_below1, soon_below1, 2),
        (below2, late_below2, soon_below2, 3),
    )

    barrier = pltpu.get_barrier_semaphore()

    def greet(peer):
        pl.semaphore_signal(barrier, inc=1, device_id=peer, device_id_type=MESH)

    def col_at(d):
        return lax.rem(c + d, col_count)

    order = sorted(range(1, col_count), key=lambda d: -min(d, col_count - d))

    def turn_of(col):
        return jnp.where(2 * col <= col_count, 2 * col, 2 * (col_count - col) + 3)

    by_turn = sorted(range(col_count), key=lambda p: 2 * p if 2 * p <= col_count else 2 * (col_count - p) + 3)
    turn = turn_of(c)

    def distance(p):
        return lax.rem(p - c + col_count, col_count)

    @pl.when(wide_above1)
    def _():
        for p in by_turn:
            pl.when(turn_of(p) > turn)(functools.partial(greet, (b, p)))

    @pl.when(jnp.logical_not(wide_above1))
    def _():
        for d in order:
            greet((b, col_at(d)))

    for i, (peer, late, _, _) in enumerate(neighbours):
        if i == 2:
            late = next_below1
        pl.when(late)(functools.partial(greet, peer))

    @pl.when(last_below1)
    def _():
        for d in range(col_count):
            greet((b - 1, col_at(d)))

    refl_copy = pltpu.make_async_copy(refl_hbm, vrec.at[c], local_sems.at[0])
    off_copy = pltpu.make_async_copy(off_hbm, off_ref, local_sems.at[1])
    x_copy = pltpu.make_async_copy(x_hbm, xe.at[WIDTH : WIDTH + rows, 0:cols], local_sems.at[2])
    refl_copy.start()
    off_copy.start()
    x_copy.start()

    xe[:, cols:wide] = jnp.zeros((WIDTH + rows, LANES), F32)
    unit = lax.broadcasted_iota(jnp.int32, (RIM, LANES), 0) == lax.broadcasted_iota(
        jnp.int32, (RIM, LANES), 1
    )
    rim = jnp.concatenate([jnp.zeros((RIM, cols), F32), jnp.where(unit, 1.0, 0.0)], axis=1)

    @pl.when(b == 0)
    def _():
        xe[0:WIDTH, 0:cols] = jnp.zeros((WIDTH, cols), F32)

    @pl.when(b == row_count - 1)
    def _():
        orec[...] = jnp.zeros((RIM, wide), F32)

    @pl.when(b >= row_count - 2)
    def _():
        o2rec[...] = jnp.zeros((EARLY, cols), F32)

    sooner = 0
    for p in by_turn:
        sooner = sooner + (turn_of(p) < turn).astype(jnp.int32)
    greeted = jnp.where(wide_above1, sooner + col_count - 1, col_count - 1)
    for _, _, soon, _ in neighbours:
        greeted = greeted + soon.astype(jnp.int32)
    pl.semaphore_wait(barrier, greeted)

    refl_copy.wait()
    gathers = [
        pltpu.make_async_remote_copy(
            src_ref=vrec.at[c], dst_ref=vrec.at[c], send_sem=send_sems.at[d], recv_sem=recv_sems.at[d],
            device_id=(b, col_at(d)), device_id_type=MESH,
        )
        for d in order
    ]

    def gather_to(p):
        return pltpu.make_async_remote_copy(
            src_ref=vrec.at[c], dst_ref=vrec.at[c],
            send_sem=send_sems.at[distance(p)], recv_sem=recv_sems.at[distance(p)],
            device_id=(b, p), device_id_type=MESH,
        )

    def answer(p):
        gather_to(p).start()
        pl.semaphore_signal(
            answered.at[col_count - distance(p)], inc=1, device_id=(b, p), device_id_type=MESH
        )

    def follow(p):
        pl.semaphore_wait(answered.at[distance(p)], 1)
        gather_to(p).start()

    @pl.when(wide_above1)
    def _():
        for p in by_turn:
            pl.when(turn_of(p) < turn)(functools.partial(answer, p))

    @pl.when(jnp.logical_not(wide_above1))
    def _():
        for copy in gathers:
            copy.start()

    def edge(i, src, dst, peer):
        return pltpu.make_async_remote_copy(
            src_ref=src, dst_ref=dst, send_sem=edge_send.at[i], recv_sem=edge_recv.at[i],
            device_id=peer, device_id_type=MESH,
        )

    halo_copy = edge(0, x_hbm.at[rows - WIDTH : rows, :], xe.at[0:WIDTH, 0:cols], above1)
    tails_copy = edge(1, vrec.at[:, :, rows - LANES : rows], tails, above1)
    tail_copies = [
        pltpu.make_async_remote_copy(
            src_ref=vrec.at[c, :, rows - LANES : rows], dst_ref=tails.at[c],
            send_sem=tail_send.at[d], recv_sem=tail_recv.at[d],
            device_id=(b + 1, col_at(d)), device_id_type=MESH,
        )
        for d in range(col_count)
    ]
    heads_copy = edge(2, vv.at[:, 0:LANES], heads, below1)
    near_copy = edge(3, osend.at[:, 0:cols], orec.at[:, 0:cols], below1)
    early = RIM - EARLY
    reply_copy = edge(5, osend.at[early:RIM, cols:wide], orec.at[early:RIM, cols:wide], below1)
    far_copy = edge(4, fsend, o2rec, below2)

    def tell(i, peer):
        pl.semaphore_signal(ready.at[i], inc=1, device_id=peer, device_id_type=MESH)

    for peer, _, soon, i in neighbours:
        if i != 3:
            pl.when(soon)(functools.partial(tell, (i + 2) % 4, peer))

    def heard(i):
        pl.semaphore_wait(ready.at[i], 1)

    @pl.when(wide_above1)
    def _():
        for copy in tail_copies:
            copy.start()

    pl.when(soon_above1)(halo_copy.start)

    @pl.when(wide_above1)
    def _():
        for p in by_turn:
            pl.when(turn_of(p) > turn)(functools.partial(follow, p))


    off_copy.wait()
    for copy in gathers:
        copy.wait_recv()
    for i in range(col_count):
        vv[i * per : (i + 1) * per, :] = vrec[i]

    pl.when(soon_below1)(heads_copy.start)

    pl.when(soon_above1 & jnp.logical_not(wide_above1))(tails_copy.start)

    def send_up():
        heard(0)
        tails_copy.start()
        halo_copy.start()

    slow_above1 = late_above1 & (place == TURN // 2 - 1)
    pl.when(late_above1 & jnp.logical_not(slow_above1))(send_up)

    sweep_of = lax.broadcasted_iota(jnp.int32, (SWEEPS, LANES), 0)
    lane_of = lax.broadcasted_iota(jnp.int32, (SWEEPS, LANES), 1)
    first = jnp.zeros((SWEEPS, LANES), jnp.int32)
    for s in range(SWEEPS):
        first = jnp.where(sweep_of == s, off_ref[s], first)
    window = (lane_of >= first) & (lane_of < first + WIDTH)

    def inner_frames():
        own = vv[...]
        turned = pltpu.roll(own, rows - WIDTH, 1)
        frames = []
        for k in range(chains - 1):
            lo = WIDTH * k
            v = own[:, lo : lo + LANES] if k % 2 == 0 else turned[:, lo - WIDTH : lo - WIDTH + LANES]
            frames.append(scaled_rows(jnp.where(window, v, 0.0)))
        return [v for v, _ in frames], [tau for _, tau in frames]

    def upper_frame():
        v = jnp.concatenate([vv[:, rows - WIDTH : rows], heads[:, 0:WIDTH]], axis=1)
        v = jnp.where(window & ((lane_of < WIDTH) | has_above1), v, 0.0)
        return scaled_rows(v)

    def keep(products):
        single[...] = products[chains - 2][0:FRAME]
        for i, k in enumerate(range(chains - 3, 0, -2)):
            pairs[i] = paired(products[k], products[k - 1])

    def run_upper(product):
        raw = xe[top : top + WIDTH, :]
        upper[...] = raw - dot(product[0:WIDTH, 0:FRAME], jnp.concatenate([raw, rim], axis=0))

    top = rows
    x_copy.wait()

    prompt = lax.rem(b, 2) == 0

    @pl.when(prompt)
    def _():
        pl.when(has_above1)(heads_copy.wait_recv)
        frames, taus = inner_frames()
        v, tau = upper_frame()
        frames, taus = frames + [v], taus + [tau]
        half = chains // 2
        products = [p for _, p in combined(frames[:half], taus[:half]) + combined(frames[half:], taus[half:])]
        run_upper(products[chains - 1])
        keep(products)

    @pl.when(jnp.logical_not(prompt))
    def _():
        keep([product for _, product in combined(*inner_frames())])

    @pl.when(next_below1)
    def _():
        heard(2)
        heads_copy.start()

    frame = jnp.concatenate([xe[top - WIDTH : top, :], rim], axis=0)
    frame = frame - dot(single[:, 0:FRAME], frame)
    xe[top - WIDTH : top, :] = frame[0:WIDTH]
    above = frame[WIDTH:FRAME]
    span = WIDTH + FRAME
    for i, k in enumerate(range(chains - 3, 0, -2)):
        lo = WIDTH * k
        frame = xe[lo : lo + span, :]
        xe[lo : lo + span, :] = frame - dot(pairs[i], frame)

    def send_far():
        pl.when(next_below2)(lambda: heard(3))
        pl.when(soon_below2 | next_below2)(far_copy.start)

    def set_far():
        fsend[...] = xe[WIDTH : WIDTH + EARLY, 0:cols] + dot(
            xe[WIDTH : WIDTH + EARLY, cols : cols + RIM], xe[top : top + RIM, 0:cols]
        )

    def set_near():
        flow = jnp.concatenate(
            [xe[WIDTH : WIDTH + RIM, 0:cols], jnp.zeros((RIM, LANES), F32)], axis=1
        ) + dot(xe[WIDTH : WIDTH + RIM, cols : cols + RIM], upper[0:RIM, :])
        osend[...] = flow

    near_now = soon_below1 | next_below1

    @pl.when(prompt)
    def _():
        set_far()
        set_near()
        pl.when(near_now)(reply_copy.start)
        send_far()
        pl.when(near_now)(near_copy.start)

    @pl.when(jnp.logical_not(prompt))
    def _():
        set_far()
        send_far()
        pl.when(slow_above1)(send_up)
        pl.when(has_above1)(heads_copy.wait_recv)
        v, tau = upper_frame()
        ((_, product),) = combined([v], [tau])
        run_upper(product)
        set_near()

        @pl.when(near_now)
        def _():
            reply_copy.start()
            near_copy.start()

    carried = jnp.concatenate([xe[WIDTH + RIM : top, :], above], axis=0)
    xe[WIDTH : WIDTH + RIM, :] = osend[...]
    moved = dot(carried[:, cols : cols + RIM], upper[0:RIM, :])
    xe[WIDTH + RIM : top + RIM, 0:cols] = carried[:, 0:cols] + moved[:, 0:cols]
    xe[WIDTH + RIM : top + RIM, cols:wide] = moved[:, cols:wide]
    xe[top + RIM : top + WIDTH, :] = upper[RIM:WIDTH, :]

    def lower_chain():
        pl.when(has_below1 & jnp.logical_not(last_below1))(tails_copy.wait_recv)

        @pl.when(last_below1)
        def _():
            for copy in tail_copies:
                copy.wait_recv()

        for i in range(col_count):
            tv[i * per : (i + 1) * per, :] = tails[i]
        v = jnp.concatenate([tv[:, WIDTH:LANES], vv[:, 0:WIDTH]], axis=1)
        v = jnp.where(window & has_below1, v, 0.0)
        dead = jnp.where(has_below1, 0.0, 1.0)
        v, tau = scaled_rows(v, dead)
        tau = jnp.where(has_below1, tau, 0.0)
        ((_, product),) = combined([v], [tau])
        first_product[...] = product[WIDTH:FRAME]


    @pl.when(jnp.logical_not(lower_last))
    def _():
        lower_chain()
        pl.when(has_below1)(halo_copy.wait_recv)
        xe[WIDTH : WIDTH + RIM, :] = xe[WIDTH : WIDTH + RIM, :] - dot(
            first_product[:, 0:FRAME], xe[0:FRAME, :]
        )

    answer = xe[WIDTH : WIDTH + rows, cols:wide]
    head = answer.astype(jnp.bfloat16).astype(F32)
    reply[...] = (
        head + pltpu.roll(head, SLOT, 1) + pltpu.roll(answer - head, 2 * SLOT, 1)
    ).astype(jnp.bfloat16)

    @pl.when(last_below1)
    def _():
        heard(2)
        heads_copy.start()
        reply_copy.start()
        near_copy.start()

    @pl.when(last_below2)
    def _():
        heard(3)
        far_copy.start()

    pl.when(has_above1)(reply_copy.wait_recv)
    pl.when(has_above2)(far_copy.wait_recv)
    passed = dot(orec[early:RIM, cols : cols + EARLY], o2rec[...])
    pl.when(has_above1)(near_copy.wait_recv)
    inflow = jnp.concatenate(
        [orec[0:early, 0:cols], orec[early:RIM, 0:cols] + passed], axis=0
    )
    head = inflow.astype(jnp.bfloat16).astype(F32)
    gap = jnp.zeros((SLOT - RIM, cols), F32)
    stack = jnp.concatenate([head, gap, inflow - head, gap, head, gap, jnp.zeros((SLOT, cols), F32)], axis=0)
    y_ref[...] = xe[WIDTH : WIDTH + rows, 0:cols] + jnp.dot(
        reply[...], stack.astype(jnp.bfloat16), preferred_element_type=F32
    )

    @pl.when(lower_last)
    def _():
        lower_chain()
        pl.when(has_below1)(halo_copy.wait_recv)
        frame = jnp.concatenate([xe[0:WIDTH, 0:cols], y_ref[0:RIM, :]], axis=0)
        y_ref[0:RIM, :] = y_ref[0:RIM, :] - dot(first_product[:, 0:FRAME], frame)

    for copy in gathers:
        copy.wait_send()

    pl.when(has_above1)(halo_copy.wait_send)
    pl.when(has_above1 & jnp.logical_not(wide_above1))(tails_copy.wait_send)

    @pl.when(wide_above1)
    def _():
        for copy in tail_copies:
            copy.wait_send()

    @pl.when(has_below1)
    def _():
        heads_copy.wait_send()
        reply_copy.wait_send()
        near_copy.wait_send()

    pl.when(has_below2)(far_copy.wait_send)


def local(row_count, col_count, eig_slab, reflectors, row_offsets):
    rows, cols = eig_slab.shape
    per = reflectors.shape[0]
    wide = cols + LANES
    return pl.pallas_call(
        functools.partial(sweep_kernel, row_count, col_count),
        out_shape=jax.ShapeDtypeStruct((rows, cols), F32),
        in_specs=[pl.BlockSpec(memory_space=pltpu.HBM)] * 3,
        out_specs=pl.BlockSpec(memory_space=pltpu.VMEM),
        scratch_shapes=[
            pltpu.SMEM((SWEEPS,), jnp.int32),
            pltpu.VMEM((WIDTH + rows, wide), F32),
            pltpu.VMEM((col_count, per, rows), F32),
            pltpu.VMEM((SWEEPS, rows), F32),
            pltpu.VMEM((SWEEPS, LANES), F32),
            pltpu.VMEM((col_count, per, LANES), F32),
            pltpu.VMEM((SWEEPS, LANES), F32),
            pltpu.VMEM((RIM, wide), F32),
            pltpu.VMEM((EARLY, cols), F32),
            pltpu.VMEM((RIM, wide), F32),
            pltpu.VMEM((EARLY, cols), F32),
            pltpu.VMEM((RIM, LANES), F32),
            pltpu.VMEM((WIDTH, wide), F32),
            pltpu.VMEM((FRAME, LANES), F32),
            pltpu.VMEM(((rows // WIDTH - 2) // 2, WIDTH + FRAME, WIDTH + FRAME), F32),
            pltpu.VMEM((rows, LANES), jnp.bfloat16),
            pltpu.SemaphoreType.DMA((3,)),
            pltpu.SemaphoreType.DMA((col_count,)),
            pltpu.SemaphoreType.DMA((col_count,)),
            pltpu.SemaphoreType.DMA((col_count,)),
            pltpu.SemaphoreType.DMA((col_count,)),
            pltpu.SemaphoreType.DMA((6,)),
            pltpu.SemaphoreType.DMA((6,)),
            pltpu.SemaphoreType.REGULAR((4,)),
            pltpu.SemaphoreType.REGULAR((col_count,)),
        ],
        compiler_params=pltpu.CompilerParams(
            collective_id=0, has_side_effects=True, vmem_limit_bytes=24 * 2**20
        ),
        name="sweep",
    )(*(pltpu.with_memory_space_constraint(a, pltpu.HBM) for a in (row_offsets, reflectors, eig_slab)))


def solution(mesh):
    placed = (P("row", "col"), P("col", "row"), P())
    return jax.shard_map(
        functools.partial(local, mesh.shape["row"], mesh.shape["col"]),
        mesh=mesh, in_specs=placed, out_specs=P("row", "col"), check_vma=False,
    )
```

```python
import functools

import jax
import jax.numpy as jnp
from jax import lax
from jax.experimental import pallas as pl
from jax.experimental.pallas import tpu as pltpu
from jax.sharding import PartitionSpec as P

WIDTH = 64
SWEEPS = 16
RIM = 24
FRAME = WIDTH + RIM
EARLY = 16
LANES = 128
SLOT = 32
TURN = 16
MESH = pl.DeviceIdType.MESH
F32 = jnp.float32
HIGH = lax.Precision.HIGH
HIGHEST = lax.Precision.HIGHEST


def dot(a, b, precision=HIGH):
    return jnp.dot(a, b, precision=precision, preferred_element_type=F32)


def halves(x):
    head = x.astype(jnp.bfloat16)
    return head, (x - head.astype(F32)).astype(jnp.bfloat16)


def scaled_rows(v, dead=0.0):
    squares = jnp.sum(v * v, axis=1, keepdims=True) + dead
    scale = lax.rsqrt(squares)
    return v * scale, 2.0 / (squares * scale * scale)


def substituted(scaled, base, w):
    half = SWEEPS // 2
    top, bottom = w[0:half], w[half:SWEEPS]
    for j in range(SWEEPS - 1):
        column = slice(base + j, base + j + 1)
        if j < half:
            row = top[j : j + 1]
            if j < half - 1:
                top = top - scaled[0:half, column] * row
        else:
            row = bottom[j - half : j - half + 1]
        bottom = bottom - scaled[half:SWEEPS, column] * row
    return jnp.concatenate([top, bottom], axis=0)


def combined(frames, taus):
    v_all = jnp.concatenate(frames, axis=0)
    tau = jnp.concatenate(taus, axis=0)
    n = v_all.shape[0]
    gram = lax.dot_general(
        v_all, v_all, (((1,), (1,)), ((), ())), precision=HIGH, preferred_element_type=F32
    )
    scaled = gram * tau
    w_all = v_all * tau
    out = []
    for i, v in enumerate(frames):
        lo = SWEEPS * i
        block = scaled[lo : lo + SWEEPS, 0:n]
        below = lax.broadcasted_iota(jnp.int32, (SWEEPS, n), 0) > (
            lax.broadcasted_iota(jnp.int32, (SWEEPS, n), 1) - lo
        )
        block = jnp.where(below, block, 0.0)
        w = substituted(block, lo, w_all[lo : lo + SWEEPS])
        vh, vl = halves(v)
        wh, wl = halves(w)
        product = lax.dot_general(
            jnp.concatenate([vh, vh, vl], axis=0), jnp.concatenate([wh, wl, wh], axis=0),
            (((0,), (0,)), ((), ())), preferred_element_type=F32,
        )
        out.append((w, product))
    return out


def paired(upper, lower):
    lanes = upper.shape[1]
    entry = lax.broadcasted_iota(jnp.int32, (RIM, lanes), 0) == lax.broadcasted_iota(
        jnp.int32, (RIM, lanes), 1
    )
    passed = jnp.where(entry, 1.0, 0.0) - upper[0:RIM]
    right = dot(lower[0:FRAME, WIDTH:FRAME], passed)
    right = jnp.concatenate([right[0:WIDTH], right[WIDTH:FRAME] + upper[0:RIM], upper[RIM:FRAME]], axis=0)
    left = jnp.concatenate([lower[0:FRAME, 0:WIDTH], jnp.zeros((WIDTH, WIDTH), F32)], axis=0)
    return jnp.concatenate([left, right[:, 0:FRAME]], axis=1)


def sweep_kernel(
    row_count, col_count,
    off_hbm, refl_hbm, x_hbm,
    y_ref,
    off_ref, xe, vrec, vv, heads, tails, tv, osend, fsend, orec, o2rec, first_product, upper, single, pairs, reply,
    local_sems, send_sems, recv_sems, tail_send, tail_recv, edge_send, edge_recv, ready, answered,
):
    per, rows = refl_hbm.shape
    cols = x_hbm.shape[1]
    wide = cols + LANES
    chains = rows // WIDTH
    b = lax.axis_index("row")
    c = lax.axis_index("col")
    below1, below2 = (b - 1, c), (b - 2, c)
    above1, above2 = (b + 1, c), (b + 2, c)
    has_below1, has_below2 = b >= 1, b >= 2
    has_above1, has_above2 = b < row_count - 1, b < row_count - 2
    place = lax.rem(b, TURN)
    late_below1 = has_below1 & ((place == 0) | (b == 1))
    late_below2 = has_below2 & ((place < 2) | (b == 2))
    late_above1 = has_above1 & (place < TURN - 1) & (b > 0)
    late_above2 = has_above2 & (place < TURN - 2) & (b > 0)
    soon_below1, soon_below2 = has_below1 & jnp.logical_not(late_below1), has_below2 & jnp.logical_not(late_below2)
    soon_above1, soon_above2 = has_above1 & jnp.logical_not(late_above1), has_above2 & jnp.logical_not(late_above2)
    last_below1, last_below2 = late_below1 & (place == 0), late_below2 & (place < 2)
    next_below1, next_below2 = late_below1 & (place > 0), late_below2 & (place > 1)
    lower_last = place == 0
    wide_above1 = soon_above1 & (place == TURN - 1)
    neighbours = (
        (above1, late_above1, soon_above1, 0),
        (above2, late_above2, soon_above2, 1),
        (below1, late_below1, soon_below1, 2),
        (below2, late_below2, soon_below2, 3),
    )

    barrier = pltpu.get_barrier_semaphore()

    def greet(peer):
        pl.semaphore_signal(barrier, inc=1, device_id=peer, device_id_type=MESH)

    def col_at(d):
        return lax.rem(c + d, col_count)

    order = sorted(range(1, col_count), key=lambda d: -min(d, col_count - d))

    def turn_of(col):
        return jnp.where(2 * col <= col_count, 2 * col, 2 * (col_count - col) + 3)

    by_turn = sorted(range(col_count), key=lambda p: 2 * p if 2 * p <= col_count else 2 * (col_count - p) + 3)
    turn = turn_of(c)

    def distance(p):
        return lax.rem(p - c + col_count, col_count)

    @pl.when(wide_above1)
    def _():
        for p in by_turn:
            pl.when(turn_of(p) > turn)(functools.partial(greet, (b, p)))

    @pl.when(jnp.logical_not(wide_above1))
    def _():
        for d in order:
            greet((b, col_at(d)))

    for i, (peer, late, _, _) in enumerate(neighbours):
        if i == 2:
            late = next_below1
        pl.when(late)(functools.partial(greet, peer))

    @pl.when(last_below1)
    def _():
        for d in range(col_count):
            greet((b - 1, col_at(d)))

    refl_copy = pltpu.make_async_copy(refl_hbm, vrec.at[c], local_sems.at[0])
    off_copy = pltpu.make_async_copy(off_hbm, off_ref, local_sems.at[1])
    x_copy = pltpu.make_async_copy(x_hbm, xe.at[WIDTH : WIDTH + rows, 0:cols], local_sems.at[2])
    refl_copy.start()
    off_copy.start()
    x_copy.start()

    xe[:, cols:wide] = jnp.zeros((WIDTH + rows, LANES), F32)
    unit = lax.broadcasted_iota(jnp.int32, (RIM, LANES), 0) == lax.broadcasted_iota(
        jnp.int32, (RIM, LANES), 1
    )
    rim = jnp.concatenate([jnp.zeros((RIM, cols), F32), jnp.where(unit, 1.0, 0.0)], axis=1)

    @pl.when(b == 0)
    def _():
        xe[0:WIDTH, 0:cols] = jnp.zeros((WIDTH, cols), F32)

    @pl.when(b == row_count - 1)
    def _():
        orec[...] = jnp.zeros((RIM, wide), F32)

    @pl.when(b >= row_count - 2)
    def _():
        o2rec[...] = jnp.zeros((EARLY, cols), F32)

    sooner = 0
    for p in by_turn:
        sooner = sooner + (turn_of(p) < turn).astype(jnp.int32)
    greeted = jnp.where(wide_above1, sooner + col_count - 1, col_count - 1)
    for _, _, soon, _ in neighbours:
        greeted = greeted + soon.astype(jnp.int32)
    pl.semaphore_wait(barrier, greeted)

    refl_copy.wait()
    gathers = [
        pltpu.make_async_remote_copy(
            src_ref=vrec.at[c], dst_ref=vrec.at[c], send_sem=send_sems.at[d], recv_sem=recv_sems.at[d],
            device_id=(b, col_at(d)), device_id_type=MESH,
        )
        for d in order
    ]

    def gather_to(p):
        return pltpu.make_async_remote_copy(
            src_ref=vrec.at[c], dst_ref=vrec.at[c],
            send_sem=send_sems.at[distance(p)], recv_sem=recv_sems.at[distance(p)],
            device_id=(b, p), device_id_type=MESH,
        )

    def answer(p):
        gather_to(p).start()
        pl.semaphore_signal(
            answered.at[col_count - distance(p)], inc=1, device_id=(b, p), device_id_type=MESH
        )

    def follow(p):
        pl.semaphore_wait(answered.at[distance(p)], 1)
        gather_to(p).start()

    @pl.when(wide_above1)
    def _():
        for p in by_turn:
            pl.when(turn_of(p) < turn)(functools.partial(answer, p))

    @pl.when(jnp.logical_not(wide_above1))
    def _():
        for copy in gathers:
            copy.start()

    def edge(i, src, dst, peer):
        return pltpu.make_async_remote_copy(
            src_ref=src, dst_ref=dst, send_sem=edge_send.at[i], recv_sem=edge_recv.at[i],
            device_id=peer, device_id_type=MESH,
        )

    halo_copy = edge(0, x_hbm.at[rows - WIDTH : rows, :], xe.at[0:WIDTH, 0:cols], above1)
    tails_copy = edge(1, vrec.at[:, :, rows - LANES : rows], tails, above1)
    tail_copies = [
        pltpu.make_async_remote_copy(
            src_ref=vrec.at[c, :, rows - LANES : rows], dst_ref=tails.at[c],
            send_sem=tail_send.at[d], recv_sem=tail_recv.at[d],
            device_id=(b + 1, col_at(d)), device_id_type=MESH,
        )
        for d in range(col_count)
    ]
    heads_copy = edge(2, vv.at[:, 0:LANES], heads, below1)
    near_copy = edge(3, osend.at[:, 0:cols], orec.at[:, 0:cols], below1)
    early = RIM - EARLY
    reply_copy = edge(5, osend.at[early:RIM, cols:wide], orec.at[early:RIM, cols:wide], below1)
    far_copy = edge(4, fsend, o2rec, below2)

    def tell(i, peer):
        pl.semaphore_signal(ready.at[i], inc=1, device_id=peer, device_id_type=MESH)

    for peer, _, soon, i in neighbours:
        if i != 3:
            pl.when(soon)(functools.partial(tell, (i + 2) % 4, peer))

    def heard(i):
        pl.semaphore_wait(ready.at[i], 1)

    @pl.when(wide_above1)
    def _():
        for copy in tail_copies:
            copy.start()

    pl.when(soon_above1)(halo_copy.start)

    @pl.when(wide_above1)
    def _():
        for p in by_turn:
            pl.when(turn_of(p) > turn)(functools.partial(follow, p))


    off_copy.wait()
    for copy in gathers:
        copy.wait_recv()
    for i in range(col_count):
        vv[i * per : (i + 1) * per, :] = vrec[i]

    pl.when(soon_below1)(heads_copy.start)

    pl.when(soon_above1 & jnp.logical_not(wide_above1))(tails_copy.start)

    def send_up():
        heard(0)
        tails_copy.start()
        halo_copy.start()

    slow_above1 = late_above1 & (place == TURN // 2 - 1)
    pl.when(late_above1 & jnp.logical_not(slow_above1))(send_up)

    sweep_of = lax.broadcasted_iota(jnp.int32, (SWEEPS, LANES), 0)
    lane_of = lax.broadcasted_iota(jnp.int32, (SWEEPS, LANES), 1)
    first = jnp.zeros((SWEEPS, LANES), jnp.int32)
    for s in range(SWEEPS):
        first = jnp.where(sweep_of == s, off_ref[s], first)
    window = (lane_of >= first) & (lane_of < first + WIDTH)

    def inner_frames():
        own = vv[...]
        turned = pltpu.roll(own, rows - WIDTH, 1)
        frames = []
        for k in range(chains - 1):
            lo = WIDTH * k
            v = own[:, lo : lo + LANES] if k % 2 == 0 else turned[:, lo - WIDTH : lo - WIDTH + LANES]
            frames.append(scaled_rows(jnp.where(window, v, 0.0)))
        return [v for v, _ in frames], [tau for _, tau in frames]

    def upper_frame():
        v = jnp.concatenate([vv[:, rows - WIDTH : rows], heads[:, 0:WIDTH]], axis=1)
        v = jnp.where(window & ((lane_of < WIDTH) | has_above1), v, 0.0)
        return scaled_rows(v)

    def keep(products):
        single[...] = products[chains - 2][0:FRAME]
        for i, k in enumerate(range(chains - 3, 0, -2)):
            pairs[i] = paired(products[k], products[k - 1])

    def run_upper(product):
        raw = xe[top : top + WIDTH, :]
        upper[...] = raw - dot(product[0:WIDTH, 0:FRAME], jnp.concatenate([raw, rim], axis=0))

    top = rows
    x_copy.wait()

    prompt = lax.rem(b, 2) == 0

    @pl.when(prompt)
    def _():
        pl.when(has_above1)(heads_copy.wait_recv)
        frames, taus = inner_frames()
        v, tau = upper_frame()
        frames, taus = frames + [v], taus + [tau]
        half = chains // 2
        products = [p for _, p in combined(frames[:half], taus[:half]) + combined(frames[half:], taus[half:])]
        run_upper(products[chains - 1])
        keep(products)

    @pl.when(jnp.logical_not(prompt))
    def _():
        keep([product for _, product in combined(*inner_frames())])

    @pl.when(next_below1)
    def _():
        heard(2)
        heads_copy.start()

    frame = jnp.concatenate([xe[top - WIDTH : top, :], rim], axis=0)
    frame = frame - dot(single[:, 0:FRAME], frame)
    xe[top - WIDTH : top, :] = frame[0:WIDTH]
    above = frame[WIDTH:FRAME]
    span = WIDTH + FRAME
    for i, k in enumerate(range(chains - 3, 0, -2)):
        lo = WIDTH * k
        frame = xe[lo : lo + span, :]
        xe[lo : lo + span, :] = frame - dot(pairs[i], frame)

    def send_far():
        pl.when(next_below2)(lambda: heard(3))
        pl.when(soon_below2 | next_below2)(far_copy.start)

    def set_far():
        fsend[...] = xe[WIDTH : WIDTH + EARLY, 0:cols] + dot(
            xe[WIDTH : WIDTH + EARLY, cols : cols + RIM], xe[top : top + RIM, 0:cols]
        )

    def set_near():
        flow = jnp.concatenate(
            [xe[WIDTH : WIDTH + RIM, 0:cols], jnp.zeros((RIM, LANES), F32)], axis=1
        ) + dot(xe[WIDTH : WIDTH + RIM, cols : cols + RIM], upper[0:RIM, :])
        osend[...] = flow

    near_now = soon_below1 | next_below1

    @pl.when(prompt)
    def _():
        set_far()
        set_near()
        pl.when(near_now)(reply_copy.start)
        send_far()
        pl.when(near_now)(near_copy.start)

    @pl.when(jnp.logical_not(prompt))
    def _():
        set_far()
        send_far()
        pl.when(slow_above1)(send_up)
        pl.when(has_above1)(heads_copy.wait_recv)
        v, tau = upper_frame()
        ((_, product),) = combined([v], [tau])
        run_upper(product)
        set_near()

        @pl.when(near_now)
        def _():
            reply_copy.start()
            near_copy.start()

    carried = jnp.concatenate([xe[WIDTH + RIM : top, :], above], axis=0)
    xe[WIDTH : WIDTH + RIM, :] = osend[...]
    moved = dot(carried[:, cols : cols + RIM], upper[0:RIM, :])
    xe[WIDTH + RIM : top + RIM, 0:cols] = carried[:, 0:cols] + moved[:, 0:cols]
    xe[WIDTH + RIM : top + RIM, cols:wide] = moved[:, cols:wide]
    xe[top + RIM : top + WIDTH, :] = upper[RIM:WIDTH, :]

    def lower_chain():
        pl.when(has_below1 & jnp.logical_not(last_below1))(tails_copy.wait_recv)

        @pl.when(last_below1)
        def _():
            for copy in tail_copies:
                copy.wait_recv()

        for i in range(col_count):
            tv[i * per : (i + 1) * per, :] = tails[i]
        v = jnp.concatenate([tv[:, WIDTH:LANES], vv[:, 0:WIDTH]], axis=1)
        v = jnp.where(window & has_below1, v, 0.0)
        dead = jnp.where(has_below1, 0.0, 1.0)
        v, tau = scaled_rows(v, dead)
        tau = jnp.where(has_below1, tau, 0.0)
        ((_, product),) = combined([v], [tau])
        first_product[...] = product[WIDTH:FRAME]


    @pl.when(jnp.logical_not(lower_last))
    def _():
        lower_chain()
        pl.when(has_below1)(halo_copy.wait_recv)
        xe[WIDTH : WIDTH + RIM, :] = xe[WIDTH : WIDTH + RIM, :] - dot(
            first_product[:, 0:FRAME], xe[0:FRAME, :]
        )

    answer = xe[WIDTH : WIDTH + rows, cols:wide]
    head = answer.astype(jnp.bfloat16).astype(F32)
    reply[...] = (
        head + pltpu.roll(head, SLOT, 1) + pltpu.roll(answer - head, 2 * SLOT, 1)
    ).astype(jnp.bfloat16)

    @pl.when(last_below1)
    def _():
        heard(2)
        heads_copy.start()
        reply_copy.start()
        near_copy.start()

    @pl.when(last_below2)
    def _():
        heard(3)
        far_copy.start()

    pl.when(has_above1)(reply_copy.wait_recv)
    pl.when(has_above2)(far_copy.wait_recv)
    passed = dot(orec[early:RIM, cols : cols + EARLY], o2rec[...])
    pl.when(has_above1)(near_copy.wait_recv)
    inflow = jnp.concatenate(
        [orec[0:early, 0:cols], orec[early:RIM, 0:cols] + passed], axis=0
    )
    head = inflow.astype(jnp.bfloat16).astype(F32)
    gap = jnp.zeros((SLOT - RIM, cols), F32)
    stack = jnp.concatenate([head, gap, inflow - head, gap, head, gap, jnp.zeros((SLOT, cols), F32)], axis=0)
    y_ref[...] = xe[WIDTH : WIDTH + rows, 0:cols] + jnp.dot(
        reply[...], stack.astype(jnp.bfloat16), preferred_element_type=F32
    )

    @pl.when(lower_last)
    def _():
        lower_chain()
        pl.when(has_below1)(halo_copy.wait_recv)
        frame = jnp.concatenate([xe[0:WIDTH, 0:cols], y_ref[0:RIM, :]], axis=0)
        y_ref[0:RIM, :] = y_ref[0:RIM, :] - dot(first_product[:, 0:FRAME], frame)

    for copy in gathers:
        copy.wait_send()

    pl.when(has_above1)(halo_copy.wait_send)
    pl.when(has_above1 & jnp.logical_not(wide_above1))(tails_copy.wait_send)

    @pl.when(wide_above1)
    def _():
        for copy in tail_copies:
            copy.wait_send()

    @pl.when(has_below1)
    def _():
        heads_copy.wait_send()
        reply_copy.wait_send()
        near_copy.wait_send()

    pl.when(has_below2)(far_copy.wait_send)


def local(row_count, col_count, eig_slab, reflectors, row_offsets):
    rows, cols = eig_slab.shape
    per = reflectors.shape[0]
    wide = cols + LANES
    return pl.pallas_call(
        functools.partial(sweep_kernel, row_count, col_count),
        out_shape=jax.ShapeDtypeStruct((rows, cols), F32),
        in_specs=[pl.BlockSpec(memory_space=pltpu.HBM)] * 3,
        out_specs=pl.BlockSpec(memory_space=pltpu.VMEM),
        scratch_shapes=[
            pltpu.SMEM((SWEEPS,), jnp.int32),
            pltpu.VMEM((WIDTH + rows, wide), F32),
            pltpu.VMEM((col_count, per, rows), F32),
            pltpu.VMEM((SWEEPS, rows), F32),
            pltpu.VMEM((SWEEPS, LANES), F32),
            pltpu.VMEM((col_count, per, LANES), F32),
            pltpu.VMEM((SWEEPS, LANES), F32),
            pltpu.VMEM((RIM, wide), F32),
            pltpu.VMEM((EARLY, cols), F32),
            pltpu.VMEM((RIM, wide), F32),
            pltpu.VMEM((EARLY, cols), F32),
            pltpu.VMEM((RIM, LANES), F32),
            pltpu.VMEM((WIDTH, wide), F32),
            pltpu.VMEM((FRAME, LANES), F32),
            pltpu.VMEM(((rows // WIDTH - 2) // 2, WIDTH + FRAME, WIDTH + FRAME), F32),
            pltpu.VMEM((rows, LANES), jnp.bfloat16),
            pltpu.SemaphoreType.DMA((3,)),
            pltpu.SemaphoreType.DMA((col_count,)),
            pltpu.SemaphoreType.DMA((col_count,)),
            pltpu.SemaphoreType.DMA((col_count,)),
            pltpu.SemaphoreType.DMA((col_count,)),
            pltpu.SemaphoreType.DMA((6,)),
            pltpu.SemaphoreType.DMA((6,)),
            pltpu.SemaphoreType.REGULAR((4,)),
            pltpu.SemaphoreType.REGULAR((col_count,)),
        ],
        compiler_params=pltpu.CompilerParams(
            collective_id=0, has_side_effects=True, vmem_limit_bytes=24 * 2**20
        ),
        name="sweep",
    )(*(pltpu.with_memory_space_constraint(a, pltpu.HBM) for a in (row_offsets, reflectors, eig_slab)))


def solution(mesh):
    placed = (P("row", "col"), P("col", "row"), P())
    return jax.shard_map(
        functools.partial(local, mesh.shape["row"], mesh.shape["col"]),
        mesh=mesh, in_specs=placed, out_specs=P("row", "col"), check_vma=False,
    )
```
